256 devices in a mesh: seq: 32 (over x_hi, z, core), ch: 8 (over y, x_lo).
Axes of the slice: x: 4 (x_hi: 2, x_lo: 2; x = x_hi * 2 + x_lo), y: 4, z: 8, core: 2. Of those that a mesh axis runs over, the one named last changes fastest.
Arguments:
- query_proj: bfloat16 [4096, 4096], P('seq', 'ch'), may hold values from -6 to 6
- key_proj: bfloat16 [4096, 4096], P('seq', 'ch'), may hold values from -6 to 6
- value_proj: bfloat16 [4096, 4096], P('seq', 'ch'), may hold values from -6 to 6
- filter_raw: float32 [4096, 4096], P('seq', 'ch'), may hold values from -6 to 6
- rates: float32 [4096], P('ch'), may hold values from 0.5 to 60
- out_weight: bfloat16 [4096, 4096], P('ch', 'seq'), may hold values from -0.09375 to 0.09375
- cotangent: bfloat16 [4096, 4096], P('seq', 'ch'), may hold values from -6 to 6
Outputs:
- grad_query: bfloat16 [4096, 4096], P('seq', 'ch')
- grad_key: bfloat16 [4096, 4096], P('seq', 'ch')
- grad_value: bfloat16 [4096, 4096], P('seq', 'ch')
- grad_filter: float32 [4096, 4096], P('seq', 'ch')
- grad_weight: float32 [4096, 4096], P('ch', 'seq')
The draws below stay inside these ranges and needn't reach their ends.
All inputs are finite; a program needn't handle non-finite values.
Results may differ from the reference program's by a relative error of at most 0.0029.
Values may be sent and summed in bfloat16 or wider, within the bound.
A program may use at most 64 MiB of HBM per device.

```python
import math
import jax
import jax.numpy as jnp
from jax import lax

D = 4096
LENGTH = 4096


def spiked(values, rng, source, target, parts, factor):
    def block_of(position):
        return (jnp.arange(values.shape[position]) // (values.shape[position] // parts)).reshape((-1,) + (1,) * (values.ndim - 1 - position))

    one_side = jax.random.permutation(rng, parts)[block_of(target)]
    second = (block_of(target) + parts // 2) % parts
    return jnp.where((block_of(source) == one_side) | (block_of(source) == second), factor * values, values)


def steps_of(key, extent, cuts, low, top_value):
    def one(position, shards_of):
        steps = jax.random.uniform(jax.random.fold_in(jax.random.fold_in(key, 6), position), (shards_of,), jnp.float32, low / len(cuts), top_value / len(cuts))
        return jnp.repeat(jnp.exp(steps), extent[position] // shards_of).reshape((-1,) + (1,) * (len(extent) - position - 1))

    loudness = one(*cuts[0])
    for cut in cuts[1:]:
        loudness = loudness * one(*cut)
    return loudness


def noise(key, dims, width, bound, cuts=(), kind=jnp.bfloat16):
    gain = steps_of(key, dims, cuts, -0.22, 0.18) if cuts else 1.0
    values = jax.random.normal(key, dims, jnp.float32) * width * gain
    return jnp.minimum(jnp.maximum(values, -bound), bound).astype(kind)


def noise_with(stream_key, dims, spread, most, pieces, heavy, held_as=jnp.bfloat16):
    entries = spread * jax.random.normal(stream_key, dims, jnp.float32)
    if pieces:
        entries = entries * steps_of(stream_key, dims, pieces, -0.22, 0.18)
    return jnp.clip(spiked(entries, jax.random.fold_in(stream_key, 3), *heavy), -most, most).astype(held_as)


def setup_inputs(seed: int = 0) -> dict:
    streams_of = jax.random.split(jax.random.key(seed), 8)
    query_proj = noise(streams_of[0], (LENGTH, D), 1.0, 6.0, ((0, 32), (1, 8)))
    key_proj = noise(streams_of[1], (LENGTH, D), 1.0, 6.0, ((0, 32), (1, 8)))
    value_proj = noise(streams_of[2], (LENGTH, D), 1.0, 6.0, ((0, 32), (1, 8)))
    filter_raw = noise(streams_of[3], (LENGTH, D), 1.0, 6.0, ((0, 32), (1, 8)), jnp.float32)
    rates = jnp.clip(jnp.exp(math.log(60.0) - 4.787492 * jax.random.uniform(streams_of[4], (D,), jnp.float32) ** steps_of(streams_of[4], (D,), ((0, 8),), -0.2, 0.2)), 0.5, 60.0)
    out_weight = noise(streams_of[5], (D, D), D ** -0.5, 0.09375, ((0, 8), (1, 32)))
    cotangent = noise_with(streams_of[6], (LENGTH, D), 1.0, 6.0, ((0, 32), (1, 8)), (0, 1, 32, 2.75))
    return dict(query_proj=query_proj, key_proj=key_proj, value_proj=value_proj, filter_raw=filter_raw, rates=rates, out_weight=out_weight, cotangent=cotangent)


def envelope_of(rates):
    positions = jnp.arange(LENGTH, dtype=jnp.int32).astype(jnp.float32) / LENGTH
    scaling = jnp.sqrt(2.0 * rates / (LENGTH * (1.0 - jnp.exp(-2.0 * rates))))
    return jnp.exp(-positions[:, None] * rates[None, :]) * scaling[None, :]

def convolve_block(operands):
    product, filt, grad_mixed = operands
    padded = 2 * LENGTH
    spec_product = jnp.fft.rfft(product, n=padded, axis=0)
    spec_filter = jnp.fft.rfft(filt, n=padded, axis=0)
    spec_grad = jnp.fft.rfft(grad_mixed, n=padded, axis=0)
    mixed = jnp.fft.irfft(spec_product * spec_filter, n=padded, axis=0)[:LENGTH]
    grad_product = jnp.fft.irfft(spec_grad * jnp.conj(spec_filter), n=padded, axis=0)[:LENGTH]
    grad_taps = jnp.fft.irfft(spec_grad * jnp.conj(spec_product), n=padded, axis=0)[:LENGTH]
    return (mixed, grad_product, grad_taps)

def reference(query_proj, key_proj, value_proj, filter_raw, rates, out_weight, cotangent):
    block_width = 512 if D % 512 == 0 else D
    block_count = D // block_width

    def split_blocks(array):
        return array.reshape(LENGTH, block_count, block_width).transpose(1, 0, 2)

    def join_blocks(array):
        return array.transpose(1, 0, 2).reshape(LENGTH, D)
    query_wide = query_proj.astype(jnp.float32)
    key_wide = key_proj.astype(jnp.float32)
    value_wide = value_proj.astype(jnp.float32)
    product = key_wide * value_wide
    envelope = envelope_of(rates)
    filt = filter_raw * envelope
    grad_gated = jnp.dot(cotangent, out_weight.T, preferred_element_type=jnp.float32)
    grad_mixed = query_wide * grad_gated
    mixed, grad_product, grad_taps = lax.map(convolve_block, (split_blocks(product), split_blocks(filt), split_blocks(grad_mixed)))
    mixed = join_blocks(mixed)
    grad_product = join_blocks(grad_product)
    grad_taps = join_blocks(grad_taps)
    gated = (query_wide * mixed).astype(jnp.bfloat16)
    grad_query = (mixed * grad_gated).astype(jnp.bfloat16)
    grad_key = (grad_product * value_wide).astype(jnp.bfloat16)
    grad_value = (grad_product * key_wide).astype(jnp.bfloat16)
    grad_filter = grad_taps * envelope
    grad_weight = jnp.dot(gated.T, cotangent, preferred_element_type=jnp.float32)
    return (grad_query, grad_key, grad_value, grad_filter, grad_weight)
```

```python
import math

import jax
import jax.numpy as jnp
import numpy as np
from jax import lax
from jax.sharding import PartitionSpec as P

PREC = lax.Precision.HIGH


def transform_tables(parts, rows):
    total = 2 * parts * rows
    k1 = np.arange(parts + 1)[:, None]
    n1 = np.arange(parts)[None, :]
    turn = 2 * math.pi * ((k1 * n1) % (2 * parts)) / (2 * parts)
    outer = np.concatenate([np.cos(turn), -np.sin(turn)], 0)
    weight = np.full((parts + 1, 1), 2.0)
    weight[0] = weight[-1] = 1.0
    outer_back = np.concatenate([weight * np.cos(turn), -weight * np.sin(turn)], 0).T / total
    n2 = np.arange(rows)
    twist = 2 * math.pi * (k1 * n2[None, :]) / total
    inner = 2 * math.pi * ((n2[:, None] * n2[None, :]) % rows) / rows
    cos, sin = np.cos(inner), np.sin(inner)
    ahead = np.block([[cos, -sin], [sin, cos]])
    back = np.block([[cos, sin], [-sin, cos]])
    return tuple(
        np.asarray(a, np.float32)
        for a in (outer, outer_back, np.cos(twist), np.sin(twist), ahead, back)
    )


def forward(x, tables):
    outer, _, tc, ts, ahead, _ = tables
    parts, c, rows = x.shape
    y = jnp.einsum("kp,pcn->kcn", outer, x, precision=PREC)
    re, im = y[: parts + 1], y[parts + 1 :]
    tc, ts = tc[:, None, :], ts[:, None, :]
    z = jnp.concatenate([re * tc + im * ts, im * tc - re * ts], -1)
    z = jnp.einsum("kcn,nm->kcm", z, ahead, precision=PREC)
    return z[..., :rows], z[..., rows:]


def inverse(re, im, tables):
    _, outer_back, tc, ts, _, back = tables
    rows = re.shape[-1]
    z = jnp.einsum("kcn,nm->kcm", jnp.concatenate([re, im], -1), back, precision=PREC)
    re, im = z[..., :rows], z[..., rows:]
    tc, ts = tc[:, None, :], ts[:, None, :]
    z = jnp.concatenate([re * tc - im * ts, im * tc + re * ts], 0)
    return jnp.einsum("pk,kcn->pcn", outer_back, z, precision=PREC)


def exchange(x):
    return lax.all_to_all(x, "seq", 0, 0, tiled=True)


def on_device(query, key, value, filter_raw, rates, out_weight, cotangent):
    rows, chans = query.shape
    parts = lax.axis_size("seq")
    fine = chans // parts
    total = rows * parts
    tables = transform_tables(parts, rows)
    offset = lax.axis_index("seq") * rows
    positions = (offset + jnp.arange(rows, dtype=jnp.int32)).astype(jnp.float32) / total
    scaling = jnp.sqrt(2.0 * rates / (total * (1.0 - jnp.exp(-2.0 * rates))))
    envelope = jnp.exp(-rates[:, None] * positions[None, :]) * scaling[:, None]

    def spread(x):
        return exchange(x.reshape(parts, fine, rows))

    key_t = key.T.astype(jnp.float32)
    value_t = value.T.astype(jnp.float32)
    query_t = query.T
    product = spread(key_t * value_t)
    filt = spread(filter_raw.T * envelope)
    query_c = spread(query_t)
    wide_cot = lax.all_gather(cotangent, "ch", axis=1, tiled=True)
    wide_weight = lax.all_gather(out_weight, "seq", axis=1, tiled=True)
    grad_gated = lax.dot_general(
        wide_weight, wide_cot, (((1,), (1,)), ((), ())), preferred_element_type=jnp.float32
    )
    grad_mixed = spread(query_t.astype(jnp.float32) * grad_gated)
    tall_cot = exchange(wide_cot.reshape(rows, parts, -1).transpose(1, 0, 2))

    pr, pi = forward(product, tables)
    fr, fi = forward(filt, tables)
    mixed = inverse(pr * fr - pi * fi, pr * fi + pi * fr, tables)
    gated = (query_c.astype(jnp.float32) * mixed).astype(jnp.bfloat16)
    all_gated = lax.all_gather(gated, "seq", axis=0)
    gr, gi = forward(grad_mixed, tables)
    grad_product = inverse(gr * fr + gi * fi, gi * fr - gr * fi, tables)
    grad_taps = inverse(gr * pr + gi * pi, gi * pr - gr * pi, tables)

    def home(x):
        return exchange(x).reshape(chans, rows)

    mixed_h = home(mixed)
    grad_product_h = home(grad_product)
    grad_taps_h = home(grad_taps)
    grad_query = (mixed_h * grad_gated).astype(jnp.bfloat16).T
    grad_key = (grad_product_h * value_t).astype(jnp.bfloat16).T
    grad_value = (grad_product_h * key_t).astype(jnp.bfloat16).T
    grad_filter = (grad_taps_h * envelope).T
    grad_weight = jnp.einsum(
        "sptr,pro->sto", all_gated.transpose(0, 1, 2, 3), tall_cot, preferred_element_type=jnp.float32
    ).reshape(chans, -1)
    return (grad_query, grad_key, grad_value, grad_filter, grad_weight)


def solution(mesh):
    return jax.shard_map(
        on_device,
        mesh=mesh,
        in_specs=(
            P("seq", "ch"),
            P("seq", "ch"),
            P("seq", "ch"),
            P("seq", "ch"),
            P("ch"),
            P("ch", "seq"),
            P("seq", "ch"),
        ),
        out_specs=(P("seq", "ch"), P("seq", "ch"), P("seq", "ch"), P("seq", "ch"), P("ch", "seq")),
        check_vma=False,
    )
```

```python
import math

import jax
import jax.numpy as jnp
import numpy as np
from jax import lax
from jax.experimental import pallas as pl
from jax.experimental.pallas import tpu as pltpu
from jax.sharding import PartitionSpec as P

PREC = lax.Precision.HIGH
MESH = pl.DeviceIdType.MESH
F32 = jnp.float32
BF16 = jnp.bfloat16
NZ, NY, PARTS, WIDE = 8, 4, 32, 8


def transform_tables(parts, rows):
    total = 2 * parts * rows
    k1 = np.arange(parts + 1)[:, None]
    n1 = np.arange(parts)[None, :]
    turn = 2 * math.pi * ((k1 * n1) % (2 * parts)) / (2 * parts)
    outer = np.concatenate([np.cos(turn), -np.sin(turn)], 0)
    weight = np.full((parts + 1, 1), 2.0)
    weight[0] = weight[-1] = 1.0
    outer_back = np.concatenate([weight * np.cos(turn), -weight * np.sin(turn)], 0).T / total
    n2 = np.arange(rows)
    twist = 2 * math.pi * (k1 * n2[None, :]) / total
    inner = 2 * math.pi * ((n2[:, None] * n2[None, :]) % rows) / rows
    cos, sin = np.cos(inner), np.sin(inner)
    ahead = np.block([[cos, -sin], [sin, cos]])
    back = np.block([[cos, sin], [-sin, cos]])
    return tuple(
        np.asarray(a, np.float32)
        for a in (outer, outer_back, np.cos(twist), np.sin(twist), ahead, back)
    )


def forward(x, tables):
    outer, _, tc, ts, ahead, _ = tables
    parts, c, rows = x.shape
    y = jnp.einsum("kp,pcn->kcn", outer, x, precision=PREC)
    re, im = y[: parts + 1], y[parts + 1 :]
    tc, ts = tc[:, None, :], ts[:, None, :]
    z = jnp.concatenate([re * tc + im * ts, im * tc - re * ts], -1)
    z = jnp.einsum("kcn,nm->kcm", z, ahead, precision=PREC)
    return z[..., :rows], z[..., rows:]


def inverse(re, im, tables):
    _, outer_back, tc, ts, _, back = tables
    rows = re.shape[-1]
    z = jnp.einsum("kcn,nm->kcm", jnp.concatenate([re, im], -1), back, precision=PREC)
    re, im = z[..., :rows], z[..., rows:]
    tc, ts = tc[:, None, :], ts[:, None, :]
    z = jnp.concatenate([re * tc - im * ts, im * tc + re * ts], 0)
    return jnp.einsum("pk,kcn->pcn", outer_back, z, precision=PREC)


class Wire:
    def __init__(self, send, recv):
        self.send, self.recv, self.made = send, recv, []

    def go(self, src, dst, to, there=None):
        i = len(self.made)
        copy = pltpu.make_async_remote_copy(
            src_ref=src,
            dst_ref=dst,
            send_sem=self.send.at[i],
            recv_sem=self.recv.at[i if there is None else there],
            device_id=to,
            device_id_type=MESH,
        )
        copy.start()
        self.made.append(copy)
        return copy

    def drain(self):
        for copy in self.made:
            copy.wait_send()


def place(x, z, k):
    return x * 16 + lax.rem(z + NZ, NZ) * 2 + k


def gather_seq(wire, buf, x, z, k):
    rows = buf.shape[1]
    half, quarter = rows // 2, rows // 4
    low, high, full = (0, half), (half, half), (0, rows)

    def send(src_x, src_z, part, dst):
        ref = buf.at[place(src_x, src_z, k), pl.ds(*part)]
        return wire.go(ref, ref, {"seq": place(*dst)})

    sib, par, right, left = (x, z, 1 - k), (1 - x, z, k), (x, z + 1, k), (x, z - 1, k)
    other = 1 - x
    siblings, across = [], []
    r = send(x, z, full, right)
    l = send(x, z, full, left)
    first = send(x, z, full, par)
    siblings.append(send(x, z, full, sib))
    yield
    first.wait_recv()
    pr = send(other, z, low, right)
    pl_ = send(other, z, low, left)
    siblings.append(send(other, z, full, sib))
    yield
    for j in (1, 2, 3):
        r.wait_recv()
        r = send(x, z - j, full if j < 3 else low, right)
        across.append((z - j, send(x, z - j, high, par)))
        siblings.append(send(x, z - j, full, sib))
        l.wait_recv()
        l = send(x, z + j, full if j < 3 else high, left)
        across.append((z + j, send(x, z + j, high, par)))
        siblings.append(send(x, z + j, full, sib))
        pr.wait_recv()
        pr = send(other, z - j, low if j < 3 else (0, quarter), right)
        siblings.append(send(other, z - j, low, sib))
        pl_.wait_recv()
        pl_ = send(other, z + j, low if j < 3 else (quarter, quarter), left)
        siblings.append(send(other, z + j, low, sib))
        yield
    l.wait_recv()
    across.append((z + 4, send(x, z + 4, high, par)))
    siblings.append(send(x, z + 4, high, sib))
    r.wait_recv()
    siblings.append(send(x, z + 4, low, sib))
    pr.wait_recv()
    pl_.wait_recv()
    siblings.append(send(other, z + 4, low, sib))
    yield
    for far, copy in across:
        copy.wait_recv()
        siblings.append(send(other, far, high, sib))
    yield
    for copy in siblings:
        copy.wait_recv()
    yield


def gather_ch(wire, buf, y, x):
    half = buf.shape[1] // 2

    def send(src_y, src_x, part, dst_y, dst_x):
        ref = buf.at[lax.rem(src_y + NY, NY) * 2 + src_x, pl.ds(*part)]
        return wire.go(ref, ref, {"ch": lax.rem(dst_y + NY, NY) * 2 + dst_x})

    full, low, high = (0, 2 * half), (0, half), (half, half)
    first = send(y, x, full, y, 1 - x)
    near = [send(y, x, full, y + 1, x), send(y, x, full, y - 1, x)]
    yield
    first.wait_recv()
    near += [send(y, 1 - x, full, y + 1, x), send(y, 1 - x, full, y - 1, x)]
    yield
    far = []
    for i, copy in enumerate(near):
        copy.wait_recv()
        whose = x if i < 2 else 1 - x
        if i % 2 == 0:
            far.append(send(y - 1, whose, low, y + 1, x))
        else:
            far.append(send(y + 1, whose, high, y - 1, x))
    yield
    for copy in far:
        copy.wait_recv()
    yield


def advance(steps, count=1):
    for _ in range(count):
        next(steps, None)


def finish(steps):
    for _ in steps:
        pass


class Swap:
    def __init__(self, src, dst, send, recv, me):
        self.src, self.dst, self.send, self.recv, self.me = src, dst, send, recv, me

    def copy(self, d):
        target = lax.rem(self.me + d, PARTS)
        return pltpu.make_async_remote_copy(
            src_ref=self.src.at[target],
            dst_ref=self.dst.at[self.me],
            send_sem=self.send.at[d],
            recv_sem=self.recv.at[d],
            device_id={"seq": target},
            device_id_type=MESH,
        )

    def start(self):
        @pl.loop(1, PARTS)
        def _(d):
            self.copy(d).start()

        self.dst[self.me] = self.src[self.me]

    def wait(self):
        @pl.loop(1, PARTS)
        def _(d):
            self.copy(d).wait()


def envelope_of(rates, me, rows):
    total = rows * PARTS
    spot = me * rows + lax.broadcasted_iota(jnp.int32, (rows, 1), 0)
    spot = spot.astype(F32) / total
    scaling = jnp.sqrt(2.0 * rates / (total * (1.0 - jnp.exp(-2.0 * rates))))
    return jnp.exp(-spot * rates) * scaling


def greet(me, extra):
    barrier = pltpu.get_barrier_semaphore()

    @pl.loop(1, PARTS)
    def _(d):
        pl.semaphore_signal(
            barrier, inc=1, device_id={"seq": lax.rem(me + d, PARTS)}, device_id_type=MESH
        )

    for to in extra:
        pl.semaphore_signal(barrier, inc=1, device_id=to, device_id_type=MESH)
    pl.semaphore_wait(barrier, PARTS - 1 + len(extra))


def opening(
    q_ref, k_ref, v_ref, f_ref, rates_ref, w_ref, c_ref,
    pf_out, gm_out, q_out, gg_out, tall,
    wbuf, cbuf, pf_src, gm_src, q_src,
    wire_send, wire_recv, swap_send, swap_recv,
):
    me, ch = lax.axis_index("seq"), lax.axis_index("ch")
    x, z, k = me // 16, lax.rem(me // 2, NZ), lax.rem(me, 2)
    y, xl = ch // 2, lax.rem(ch, 2)
    rows, chans = q_ref.shape
    fine = chans // PARTS
    wire = Wire(wire_send, wire_recv)

    wbuf[me] = w_ref[...]
    cbuf[ch] = c_ref[...]
    keeper = lax.rem(me // 4 + 1 + lax.rem(me, 4), WIDE)
    targets = [{"seq": ch * 4 + i, "ch": keeper} for i in range(4)]
    sources = [
        {"seq": 4 * lax.rem(ch - 1 - j + WIDE, WIDE) + j, "ch": me // 4} for j in range(4)
    ]
    around = [
        {"ch": y * 2 + 1 - xl},
        {"ch": lax.rem(y + 1, NY) * 2 + xl},
        {"ch": lax.rem(y + NY - 1, NY) * 2 + xl},
    ]
    greet(me, targets + sources + around)

    weights = gather_seq(wire, wbuf, x, z, k)
    advance(weights)
    wide = gather_ch(wire, cbuf, y, xl)
    advance(wide)
    base = len(wire.made)
    for i, to in enumerate(targets):
        src = cbuf.at[ch, :, pl.ds(i * 128, 128)]
        wire.go(src, tall.at[keeper, lax.rem(me, 4)], to, base + lax.rem(me, 4))

    env = envelope_of(rates_ref[...], me, rows)
    product = k_ref[...].astype(F32) * v_ref[...].astype(F32)
    pf_src[:, 0] = product.T.reshape(PARTS, fine, rows)
    pf_src[:, 1] = (f_ref[...] * env).T.reshape(PARTS, fine, rows)
    q_src[...] = q_ref[...].astype(F32).T.reshape(PARTS, fine, rows).astype(BF16)

    advance(weights)
    advance(wide)
    advance(weights)
    advance(wide)
    for j in range(4):
        pltpu.make_async_copy(tall.at[0, 0], tall.at[0, 0], wire_recv.at[base + j]).wait()
    high = gather_ch(wire, tall, y, xl)
    advance(high)
    advance(weights)
    advance(wide)
    advance(high)
    advance(weights)
    pf = Swap(pf_src, pf_out, swap_send.at[0], swap_recv.at[0], me)
    qs = Swap(q_src, q_out, swap_send.at[1], swap_recv.at[1], me)
    gm = Swap(gm_src, gm_out, swap_send.at[2], swap_recv.at[2], me)
    pf.start()
    qs.start()
    advance(high)
    finish(weights)
    finish(wide)
    total = jnp.zeros((rows, chans), F32)
    for h in range(WIDE):
        part = jnp.concatenate([wbuf[4 * h + i] for i in range(4)], axis=1)
        total += lax.dot_general(
            cbuf[h], part, (((1,), (1,)), ((), ())), preferred_element_type=F32
        )
    gg_out[...] = total
    gm_src[...] = (q_ref[...].astype(F32) * total).T.reshape(PARTS, fine, rows)
    gm.start()
    finish(high)
    pf.wait()
    qs.wait()
    gm.wait()
    wire.drain()


def closing(
    gated_ref, mixed_ref, prod_ref, taps_ref, gg_ref, k_ref, v_ref, rates_ref, tall_ref,
    gq_out, gk_out, gv_out, gf_out, gw_out,
    gbuf, mixed_in, prod_in, taps_in,
    wire_send, wire_recv, swap_send, swap_recv,
):
    me = lax.axis_index("seq")
    x, z, k = me // 16, lax.rem(me // 2, NZ), lax.rem(me, 2)
    rows, chans = k_ref.shape
    fine = chans // PARTS
    wire = Wire(wire_send, wire_recv)
    gbuf[me] = gated_ref[...]
    greet(me, [])
    steps = gather_seq(wire, gbuf, x, z, k)
    advance(steps, 5)
    swaps = [
        Swap(src, dst, swap_send.at[i], swap_recv.at[i], me)
        for i, (src, dst) in enumerate(
            ((mixed_ref, mixed_in), (prod_ref, prod_in), (taps_ref, taps_in))
        )
    ]
    for swap in swaps:
        swap.start()
    env = envelope_of(rates_ref[...], me, rows)
    finish(steps)
    total = jnp.zeros(gw_out.shape, F32)
    for a in range(WIDE):
        left, right = [], []
        for j in range(4):
            block = 4 * a + j
            left.append(gbuf[:, pl.ds(block * fine, fine), :].reshape(chans, rows))
            right.append(tall_ref[(a + 1 + j) % WIDE, j])
        total += jnp.dot(
            jnp.concatenate(left, axis=1),
            jnp.concatenate(right, axis=0),
            preferred_element_type=F32,
        )
    gw_out[...] = total
    swaps[0].wait()
    gq_out[...] = (mixed_in[...].reshape(chans, rows).T * gg_ref[...]).astype(BF16)
    swaps[1].wait()
    back = prod_in[...].reshape(chans, rows).T
    gk_out[...] = (back * v_ref[...].astype(F32)).astype(BF16)
    gv_out[...] = (back * k_ref[...].astype(F32)).astype(BF16)
    swaps[2].wait()
    gf_out[...] = taps_in[...].reshape(chans, rows).T * env
    wire.drain()


def on_device(query, key, value, filter_raw, rates, out_weight, cotangent):
    rows, chans = query.shape
    fine = chans // PARTS
    tables = transform_tables(PARTS, rows)
    rates = rates.reshape(1, chans)
    vmem = pl.BlockSpec(memory_space=pltpu.VMEM)
    shape = jax.ShapeDtypeStruct
    piece = (PARTS, fine, rows)
    sems = [
        pltpu.SemaphoreType.DMA((80,)),
        pltpu.SemaphoreType.DMA((80,)),
        pltpu.SemaphoreType.DMA((3, PARTS)),
        pltpu.SemaphoreType.DMA((3, PARTS)),
    ]
    pf, gm, query_c, grad_gated, tall = pl.pallas_call(
        opening,
        out_shape=(
            shape((PARTS, 2, fine, rows), F32),
            shape(piece, F32),
            shape(piece, BF16),
            shape((rows, chans), F32),
            shape((WIDE, 4, rows, out_weight.shape[1]), BF16),
        ),
        in_specs=[vmem] * 7,
        out_specs=(vmem,) * 5,
        scratch_shapes=[
            pltpu.VMEM((PARTS, chans, out_weight.shape[1]), BF16),
            pltpu.VMEM((WIDE, rows, chans), BF16),
            pltpu.VMEM((PARTS, 2, fine, rows), F32),
            pltpu.VMEM(piece, F32),
            pltpu.VMEM(piece, BF16),
        ]
        + sems,
        compiler_params=pltpu.CompilerParams(
            collective_id=0, has_side_effects=True, vmem_limit_bytes=40 * 2**20
        ),
        name="opening",
    )(query, key, value, filter_raw, rates, out_weight, cotangent)

    pr, pi = forward(pf[:, 0], tables)
    fr, fi = forward(pf[:, 1], tables)
    gr, gi = forward(gm, tables)
    mixed = inverse(pr * fr - pi * fi, pr * fi + pi * fr, tables)
    gated = (query_c.astype(F32) * mixed).astype(BF16).reshape(chans, rows)
    grad_product = inverse(gr * fr + gi * fi, gi * fr - gr * fi, tables)
    grad_taps = inverse(gr * pr + gi * pi, gi * pr - gr * pi, tables)

    return pl.pallas_call(
        closing,
        out_shape=(
            shape((rows, chans), BF16),
            shape((rows, chans), BF16),
            shape((rows, chans), BF16),
            shape((rows, chans), F32),
            shape(out_weight.shape, F32),
        ),
        in_specs=[vmem] * 9,
        out_specs=(vmem,) * 5,
        scratch_shapes=[pltpu.VMEM((PARTS, chans, rows), BF16)] + [pltpu.VMEM(piece, F32)] * 3 + sems,
        compiler_params=pltpu.CompilerParams(
            collective_id=1, has_side_effects=True, vmem_limit_bytes=40 * 2**20
        ),
        name="closing",
    )(gated, mixed, grad_product, grad_taps, grad_gated, key, value, rates, tall)


def solution(mesh):
    return jax.shard_map(
        on_device,
        mesh=mesh,
        in_specs=(
            P("seq", "ch"),
            P("seq", "ch"),
            P("seq", "ch"),
            P("seq", "ch"),
            P("ch"),
            P("ch", "seq"),
            P("seq", "ch"),
        ),
        out_specs=(P("seq", "ch"), P("seq", "ch"), P("seq", "ch"), P("seq", "ch"), P("ch", "seq")),
        check_vma=False,
    )
```

```python
import math

import jax
import jax.numpy as jnp
import numpy as np
from jax import lax
from jax.experimental import pallas as pl
from jax.experimental.pallas import tpu as pltpu
from jax.sharding import PartitionSpec as P

MESH = pl.DeviceIdType.MESH
F32 = jnp.float32
BF16 = jnp.bfloat16
NZ, NY, PARTS, WIDE = 8, 4, 32, 8


def transform_tables(rows):
    total = 2 * PARTS * rows
    k1 = np.arange(PARTS + 1)[:, None]
    n1 = np.arange(PARTS)[None, :]
    turn = 2 * math.pi * ((k1 * n1) % (2 * PARTS)) / (2 * PARTS)
    eye = np.eye(8)
    outer = np.kron(np.concatenate([np.cos(turn), -np.sin(turn)[1:-1]], 0), eye)
    weight = np.full((PARTS + 1, 1), 2.0)
    weight[0] = weight[-1] = 1.0
    outer_back = np.concatenate([weight * np.cos(turn), (-weight * np.sin(turn))[1:-1]], 0)
    outer_back = np.kron(outer_back.T / total, eye)
    n2 = np.arange(rows)
    twist = np.repeat(2 * math.pi * (k1 * n2[None, :]) / total, 8, axis=0)
    inner = 2 * math.pi * ((n2[:, None] * n2[None, :]) % rows) / rows
    cos, sin = np.cos(inner), np.sin(inner)
    ahead = np.block([[cos, -sin], [sin, cos]])
    back = np.block([[cos, sin], [-sin, cos]])

    def pair(m):
        high = np.asarray(m, np.float32).astype(BF16)
        low = (m - high.astype(np.float64)).astype(BF16)
        return np.stack([high, low])

    turns = np.stack([np.cos(twist), np.sin(twist)]).astype(np.float32)
    return pair(outer), pair(outer_back), np.concatenate([pair(ahead), pair(back)]), turns


def halves(x):
    high = x.astype(BF16)
    return high, (x - high.astype(F32)).astype(BF16)


def dot(a, b):
    return jnp.dot(a, b, preferred_element_type=F32)


def dot_const_left(const, x):
    high, low = halves(x)
    return dot(const[0], high) + dot(const[0], low) + dot(const[1], high)


def dot_const_right(x, const, at):
    high, low = halves(x)
    return dot(high, const[at]) + dot(low, const[at]) + dot(high, const[at + 1])


def forward(signals, outer, inner, turns):
    groups = [x[:, 8 * i : 8 * i + 8, :].reshape(256, 128) for x in signals for i in range(2)]
    y = dot_const_left(outer, jnp.concatenate(groups, axis=1))
    cos, sin = turns[0], turns[1]
    rest = jnp.zeros((8, 128), F32)
    rows = []
    for i in range(len(groups)):
        part = y[:, 128 * i : 128 * i + 128]
        re, im = part[:264], jnp.concatenate([rest, part[264:], rest], axis=0)
        rows.append(jnp.concatenate([re * cos + im * sin, im * cos - re * sin], axis=1))
    z = dot_const_right(jnp.concatenate(rows, axis=0), inner, 0)
    return [(z[528 * i : 528 * i + 528, :128], z[528 * i : 528 * i + 528, 128:]) for i in range(len(signals))]


def inverse(spectra, outer_back, inner, turns):
    z = jnp.concatenate([jnp.concatenate(pair, axis=1) for pair in spectra], axis=0)
    z = dot_const_right(z, inner, 2)
    cos, sin = turns[0], turns[1]
    columns = []
    for i in range(2 * len(spectra)):
        re, im = z[264 * i : 264 * i + 264, :128], z[264 * i : 264 * i + 264, 128:]
        columns.append(jnp.concatenate([re * cos - im * sin, (im * cos + re * sin)[8:256]], axis=0))
    y = dot_const_left(outer_back, jnp.concatenate(columns, axis=1))
    groups = [y[:, 128 * i : 128 * i + 128].reshape(PARTS, 8, 128) for i in range(len(columns))]
    return [jnp.concatenate(groups[2 * i : 2 * i + 2], axis=1) for i in range(len(spectra))]


def pack(x, scale):
    x = x * scale
    square = x * x
    return (square * (x * jnp.abs(x))).astype(BF16)


def unpack(code, scale):
    code = code.astype(F32)
    size = jnp.sqrt(jnp.sqrt(jnp.abs(code))) * (1.0 / scale)
    return jnp.where(code < 0.0, -size, size)


class Wire:
    def __init__(self, send, recv):
        self.send, self.recv, self.made = send, recv, []

    def go(self, src, dst, to, there=None):
        i = len(self.made)
        copy = pltpu.make_async_remote_copy(
            src_ref=src,
            dst_ref=dst,
            send_sem=self.send.at[i],
            recv_sem=self.recv.at[i if there is None else there],
            device_id=to,
            device_id_type=MESH,
        )
        copy.start()
        self.made.append(copy)
        return copy

    def drain(self):
        for copy in self.made:
            copy.wait_send()


def place(x, z, k):
    return x * 16 + lax.rem(z + NZ, NZ) * 2 + k


def gather_seq(wire, buf, x, z, k):
    rows = buf.shape[1]
    half, quarter = rows // 2, rows // 4
    low, high, full = (0, half), (half, half), (0, rows)

    def send(src_x, src_z, part, dst):
        ref = buf.at[place(src_x, src_z, k), pl.ds(*part)]
        return wire.go(ref, ref, {"seq": place(*dst)})

    sib, par, right, left = (x, z, 1 - k), (1 - x, z, k), (x, z + 1, k), (x, z - 1, k)
    other = 1 - x
    siblings, across = [], []
    r = send(x, z, full, right)
    l = send(x, z, full, left)
    first = send(x, z, full, par)
    siblings.append(send(x, z, full, sib))
    yield
    first.wait_recv()
    pr = send(other, z, low, right)
    pl_ = send(other, z, low, left)
    siblings.append(send(other, z, full, sib))
    yield
    for j in (1, 2, 3):
        r.wait_recv()
        r = send(x, z - j, full if j < 3 else low, right)
        across.append((z - j, send(x, z - j, high, par)))
        siblings.append(send(x, z - j, full, sib))
        l.wait_recv()
        l = send(x, z + j, full if j < 3 else high, left)
        across.append((z + j, send(x, z + j, high, par)))
        siblings.append(send(x, z + j, full, sib))
        pr.wait_recv()
        pr = send(other, z - j, low if j < 3 else (0, quarter), right)
        siblings.append(send(other, z - j, low, sib))
        pl_.wait_recv()
        pl_ = send(other, z + j, low if j < 3 else (quarter, quarter), left)
        siblings.append(send(other, z + j, low, sib))
        yield
    l.wait_recv()
    across.append((z + 4, send(x, z + 4, high, par)))
    siblings.append(send(x, z + 4, high, sib))
    r.wait_recv()
    siblings.append(send(x, z + 4, low, sib))
    pr.wait_recv()
    pl_.wait_recv()
    siblings.append(send(other, z + 4, low, sib))
    yield
    for far, copy in across:
        copy.wait_recv()
        siblings.append(send(other, far, high, sib))
    yield
    for copy in siblings:
        copy.wait_recv()
    yield


def ring_z(wire, buf, x, z, k, across):
    def ref(far, *part):
        return buf.at[(lax.rem(z + far + NZ, NZ) * 2 + k, *part)]

    def send(far, part, step):
        r = ref(far, part)
        return wire.go(r, r, {"seq": place(x, z + step, k)})

    def share(far, *part):
        r = ref(far, *part)
        return wire.go(r, r, {"seq": place(x, z, 1 - k)})

    other = 1 - x
    right, left = send(0, x, 1), send(0, x, -1)
    siblings = [share(0, x)]
    yield
    across.wait_recv()
    right2, left2 = send(0, other, 1), send(0, other, -1)
    siblings.append(share(0, other))
    yield
    for j in (1, 2, 3):
        right.wait_recv()
        right = send(-j, x, 1)
        left.wait_recv()
        left = send(j, x, -1) if j < 3 else None
        right2.wait_recv()
        right2 = send(-j, other, 1) if j < 3 else None
        left2.wait_recv()
        left2 = send(j, other, -1)
        siblings += [share(-j), share(j)]
        yield
    right.wait_recv()
    left2.wait_recv()
    siblings.append(share(4))
    yield
    for copy in siblings:
        copy.wait_recv()
    yield


def gather_ch(wire, buf, y, x):
    half = buf.shape[1] // 2

    def send(src_y, src_x, part, dst_y, dst_x):
        ref = buf.at[lax.rem(src_y + NY, NY) * 2 + src_x, pl.ds(*part)]
        return wire.go(ref, ref, {"ch": lax.rem(dst_y + NY, NY) * 2 + dst_x})

    full, low, high = (0, 2 * half), (0, half), (half, half)
    first = send(y, x, full, y, 1 - x)
    near = [send(y, x, full, y + 1, x), send(y, x, full, y - 1, x)]
    yield
    first.wait_recv()
    near += [send(y, 1 - x, full, y + 1, x), send(y, 1 - x, full, y - 1, x)]
    yield
    far = []
    for i, copy in enumerate(near):
        copy.wait_recv()
        whose = x if i < 2 else 1 - x
        if i % 2 == 0:
            far.append(send(y - 1, whose, low, y + 1, x))
        else:
            far.append(send(y + 1, whose, high, y - 1, x))
    yield
    for copy in far:
        copy.wait_recv()
    yield


def advance(steps, count=1):
    for _ in range(count):
        next(steps, None)


def finish(steps):
    for _ in steps:
        pass


class Swap:
    def __init__(self, src, dst, send, recv, me):
        self.src, self.dst, self.send, self.recv, self.me = src, dst, send, recv, me

    def copy(self, d):
        target = lax.rem(self.me + d, PARTS)
        return pltpu.make_async_remote_copy(
            src_ref=self.src.at[target],
            dst_ref=self.dst.at[self.me],
            send_sem=self.send.at[d],
            recv_sem=self.recv.at[d],
            device_id={"seq": target},
            device_id_type=MESH,
        )

    def start(self, low=1, high=PARTS):
        @pl.loop(low, high)
        def _(d):
            self.copy(d).start()

        if low == 1:
            self.dst[self.me] = self.src[self.me]

    def wait(self):
        @pl.loop(1, PARTS)
        def _(d):
            self.copy(d).wait()


def envelope_of(rates, me, rows):
    total = rows * PARTS
    spot = me * rows + lax.broadcasted_iota(jnp.int32, (rows, 1), 0)
    spot = spot.astype(F32) / total
    scaling = jnp.sqrt(2.0 * rates / (total * (1.0 - jnp.exp(-2.0 * rates))))
    return jnp.exp(-spot * rates) * scaling


def whole(
    q_hbm, k_hbm, v_hbm, f_hbm, r_hbm, w_hbm, c_hbm, outer_hbm, back_hbm, inner_hbm, turns_hbm,
    gq_out, gk_out, gv_out, gf_out, gw_out,
    q_ref, k_ref, v_ref, f_ref, r_ref, outer, back, inner, turns,
    wbuf, cbuf, tall, gbuf, gg_ref, rate_ref,
    in_src, in_dst, gm_src, gm_dst, home_src, home_dst, gated_ref, half_src, half_dst,
    load_sem, wire_send, wire_recv, swap_send, swap_recv,
):
    me, ch = lax.axis_index("seq"), lax.axis_index("ch")
    x, z, k = me // 16, lax.rem(me // 2, NZ), lax.rem(me, 2)
    zk = lax.rem(me, 16)
    y, xl = ch // 2, lax.rem(ch, 2)
    rows, chans = q_ref.shape
    fine = chans // PARTS
    wire = Wire(wire_send, wire_recv)

    loads = [
        pltpu.make_async_copy(src, dst, load_sem.at[i])
        for i, (src, dst) in enumerate(
            (
                (w_hbm, wbuf.at[me]),
                (c_hbm, cbuf.at[ch]),
                (k_hbm, k_ref),
                (v_hbm, v_ref),
                (f_hbm, f_ref),
                (q_hbm, q_ref),
                (r_hbm, r_ref),
                (outer_hbm, outer),
                (back_hbm, back),
                (inner_hbm, inner),
                (turns_hbm, turns),
            )
        )
    ]
    for load in loads:
        load.start()

    spot = (ch // 4) * 16 + zk
    keeper = lax.rem(spot // 4 + 1 + lax.rem(spot, 4), WIDE)
    targets = [{"seq": x * 16 + lax.rem(ch, 4) * 4 + i, "ch": keeper} for i in range(4)]
    sources = []
    for j in range(4):
        theirs = 4 * lax.rem(ch - 1 - j + WIDE, WIDE) + j
        sources.append(
            {"seq": x * 16 + lax.rem(theirs, 16), "ch": (theirs // 16) * 4 + zk // 4}
        )
    around = [
        {"ch": y * 2 + 1 - xl},
        {"ch": lax.rem(y + 1, NY) * 2 + xl},
        {"ch": lax.rem(y + NY - 1, NY) * 2 + xl},
    ]
    greeted = targets + sources + around
    barrier = pltpu.get_barrier_semaphore()

    @pl.loop(1, PARTS)
    def _(d):
        pl.semaphore_signal(
            barrier, inc=1, device_id={"seq": lax.rem(me + d, PARTS)}, device_id_type=MESH
        )

    for to in greeted:
        pl.semaphore_signal(barrier, inc=1, device_id=to, device_id_type=MESH)

    for load in loads:
        load.wait()

    def turned(value):
        return value.T.reshape(PARTS, fine, rows)

    in_src[:, 0:16] = pack(turned(k_ref[...].astype(F32) * v_ref[...].astype(F32)), 2.0**25)
    in_src[:, 16:32] = pack(turned(f_ref[...]), 2.0**28)
    in_src[:, 32:48] = turned(q_ref[...].astype(F32)).astype(BF16)
    rate_ref[...] = jnp.broadcast_to(r_ref[...], (rows, chans)).T
    env = envelope_of(r_ref[...], me, rows)
    own_rates = rate_ref[pl.ds(me * fine, fine), :]
    lanes = lax.broadcasted_iota(jnp.int32, (fine, rows), 1)
    span = float(rows * PARTS)
    own_scaling = jnp.sqrt(2.0 * own_rates / (span * (1.0 - jnp.exp(-2.0 * own_rates))))
    envelope = jnp.stack(
        [
            jnp.exp(-((lanes + block * rows).astype(F32) / span) * own_rates) * own_scaling
            for block in range(PARTS)
        ]
    )
    pl.semaphore_wait(barrier, PARTS - 1 + len(greeted))

    weights = gather_seq(wire, wbuf, x, z, k)
    advance(weights)
    wide = gather_ch(wire, cbuf, y, xl)
    advance(wide)
    base = len(wire.made)
    for i, to in enumerate(targets):
        src = cbuf.at[ch, :, pl.ds(i * 128, 128)]
        wire.go(src, tall.at[keeper, lax.rem(me, 4)], to, base + lax.rem(me, 4))

    def swap(i, src, dst):
        return Swap(src, dst, swap_send.at[i], swap_recv.at[i], me)

    early = swap(0, in_src, in_dst)
    late = swap(1, gm_src, gm_dst)
    homes = [swap(2 + i, home_src.at[i], home_dst.at[i]) for i in range(3)]

    early.start(1, 12)
    advance(weights)
    advance(wide)
    early.start(12, 22)
    advance(weights)
    advance(wide)
    early.start(22, PARTS)
    advance(weights)
    for j in range(4):
        pltpu.make_async_copy(tall.at[0, 0], tall.at[0, 0], wire_recv.at[base + j]).wait()
    high = gather_ch(wire, tall, y, xl)
    advance(high)
    advance(weights)
    advance(wide)
    advance(high)
    advance(weights)
    advance(high)

    early.wait()
    product = unpack(in_dst[:, 0:16], 2.0**25)
    filt = unpack(in_dst[:, 16:32], 2.0**28) * envelope
    (pr, pi), (fr, fi) = forward([product, filt], outer, inner, turns)
    (mixed,) = inverse([(pr * fr - pi * fi, pr * fi + pi * fr)], back, inner, turns)
    gated_ref[...] = (in_dst[:, 32:48].astype(F32) * mixed).astype(BF16)
    across = wire.go(
        gated_ref.at[pl.ds(16 * (1 - x), 16)], gbuf.at[zk, x], {"seq": place(1 - x, z, k)}
    )
    gbuf[zk, x] = gated_ref[pl.ds(16 * x, 16)]
    ring = ring_z(wire, gbuf, x, z, k, across)
    advance(ring)
    home_src[0] = pack(mixed, 2.0**17)
    homes[0].start()

    finish(weights)
    finish(wide)
    total = jnp.zeros((rows, chans), F32)
    for h in range(WIDE):
        part = jnp.concatenate([wbuf[4 * h + i] for i in range(4)], axis=1)
        total += lax.dot_general(
            cbuf[h], part, (((1,), (1,)), ((), ())), preferred_element_type=F32
        )
    gg_ref[...] = total
    gm_src[...] = pack(turned(q_ref[...].astype(F32) * total), 2.0**17)
    late.start()
    advance(ring, 2)
    finish(high)
    late.wait()
    grad = unpack(gm_dst[...], 2.0**17)
    ((gr, gi),) = forward([grad], outer, inner, turns)
    advance(ring)
    back_product, back_taps = inverse(
        [(gr * fr + gi * fi, gi * fr - gr * fi), (gr * pr + gi * pi, gi * pr - gr * pi)],
        back, inner, turns,
    )
    home_src[1] = pack(back_product, 2.0**8)
    homes[1].start()
    home_src[2] = pack(back_taps, 1.0)
    homes[2].start()
    finish(ring)

    total = jnp.zeros((chans, 256), F32)
    for a in range(4):
        left, right = [], []
        for j in range(4):
            block = 4 * a + j
            left.append(
                jnp.concatenate([gbuf[:, i, block].reshape(256, 128) for i in range(2)], axis=0)
            )
            right.append(
                jnp.concatenate([tall[(4 * i + a + 1 + j) % WIDE, j] for i in range(2)], axis=1)
            )
        total += dot(jnp.concatenate(left, axis=1), jnp.concatenate(right, axis=0))
    mine = jnp.where(x == 0, total[:, :128], total[:, 128:])
    theirs = jnp.where(x == 0, total[:, 128:], total[:, :128])
    half_src[...] = pack(theirs, 1.0)
    last = wire.go(half_src, half_dst, {"seq": place(1 - x, z, k)})

    def arrived(i, scale):
        homes[i].wait()
        return unpack(home_dst[i].reshape(chans, rows), scale).T

    gq_out[...] = (arrived(0, 2.0**17) * gg_ref[...]).astype(BF16)
    grad_product = arrived(1, 2.0**8)
    gk_out[...] = (grad_product * v_ref[...].astype(F32)).astype(BF16)
    gv_out[...] = (grad_product * k_ref[...].astype(F32)).astype(BF16)
    gf_out[...] = arrived(2, 1.0) * env
    last.wait_recv()
    gw_out[...] = mine + unpack(half_dst[...], 1.0)
    wire.drain()


def on_device(query, key, value, filter_raw, rates, out_weight, cotangent):
    rows, chans = query.shape
    fine = chans // PARTS
    tables = transform_tables(rows)
    columns = out_weight.shape[1]
    shape = jax.ShapeDtypeStruct
    block = pltpu.VMEM((rows, chans), BF16)
    piece = (PARTS, fine, rows)
    return pl.pallas_call(
        whole,
        out_shape=(
            shape((rows, chans), BF16),
            shape((rows, chans), BF16),
            shape((rows, chans), BF16),
            shape((rows, chans), F32),
            shape(out_weight.shape, F32),
        ),
        in_specs=[pl.BlockSpec(memory_space=pl.ANY)] * 11,
        out_specs=(pl.BlockSpec(memory_space=pltpu.VMEM),) * 5,
        scratch_shapes=[
            block,
            block,
            block,
            pltpu.VMEM((rows, chans), F32),
            pltpu.VMEM((1, chans), F32),
            *(pltpu.VMEM(t.shape, t.dtype) for t in tables),
            pltpu.VMEM((PARTS, chans, columns), BF16),
            pltpu.VMEM((WIDE, rows, chans), BF16),
            pltpu.VMEM((WIDE, 4, rows, columns), BF16),
            pltpu.VMEM((16, 2, 16, fine, rows), BF16),
            pltpu.VMEM((rows, chans), F32),
            pltpu.VMEM((chans, rows), F32),
            pltpu.VMEM((PARTS, 3 * fine, rows), BF16),
            pltpu.VMEM((PARTS, 3 * fine, rows), BF16),
            pltpu.VMEM(piece, BF16),
            pltpu.VMEM(piece, BF16),
            pltpu.VMEM((3, *piece), BF16),
            pltpu.VMEM((3, *piece), BF16),
            pltpu.VMEM(piece, BF16),
            pltpu.VMEM((chans, columns), BF16),
            pltpu.VMEM((chans, columns), BF16),
            pltpu.SemaphoreType.DMA((11,)),
            pltpu.SemaphoreType.DMA((128,)),
            pltpu.SemaphoreType.DMA((128,)),
            pltpu.SemaphoreType.DMA((5, PARTS)),
            pltpu.SemaphoreType.DMA((5, PARTS)),
        ],
        compiler_params=pltpu.CompilerParams(
            collective_id=0, has_side_effects=True, vmem_limit_bytes=48 * 2**20
        ),
        name="whole",
    )(
        query, key, value, filter_raw, rates.reshape(1, chans), out_weight, cotangent,
        *(jnp.asarray(t) for t in tables),
    )


def solution(mesh):
    return jax.shard_map(
        on_device,
        mesh=mesh,
        in_specs=(
            P("seq", "ch"),
            P("seq", "ch"),
            P("seq", "ch"),
            P("seq", "ch"),
            P("ch"),
            P("ch", "seq"),
            P("seq", "ch"),
        ),
        out_specs=(P("seq", "ch"), P("seq", "ch"), P("seq", "ch"), P("seq", "ch"), P("ch", "seq")),
        check_vma=False,
    )
```

```python
import math

import jax
import jax.numpy as jnp
import numpy as np
from jax import lax
from jax.experimental import pallas as pl
from jax.experimental.pallas import tpu as pltpu
from jax.sharding import PartitionSpec as P

MESH = pl.DeviceIdType.MESH
F32 = jnp.float32
BF16 = jnp.bfloat16
NZ, NY, PARTS, WIDE = 8, 4, 32, 8


def transform_tables(rows):
    total = 2 * PARTS * rows
    k1 = np.arange(PARTS + 1)[:, None]
    n1 = np.arange(PARTS)[None, :]
    turn = 2 * math.pi * ((k1 * n1) % (2 * PARTS)) / (2 * PARTS)
    eye = np.eye(8)
    outer = np.kron(np.concatenate([np.cos(turn), -np.sin(turn)[1:-1]], 0), eye)
    weight = np.full((PARTS + 1, 1), 2.0)
    weight[0] = weight[-1] = 1.0
    outer_back = np.concatenate([weight * np.cos(turn), (-weight * np.sin(turn))[1:-1]], 0)
    outer_back = np.kron(outer_back.T / total, eye)
    n2 = np.arange(rows)
    twist = np.repeat(2 * math.pi * (k1 * n2[None, :]) / total, 8, axis=0)
    inner = 2 * math.pi * ((n2[:, None] * n2[None, :]) % rows) / rows
    cos, sin = np.cos(inner), np.sin(inner)
    ahead = np.block([[cos, -sin], [sin, cos]])
    back = np.block([[cos, sin], [-sin, cos]])

    turns = np.stack([np.cos(twist), np.sin(twist)])
    return tuple(np.asarray(m, np.float32) for m in (outer, outer_back, ahead, back, turns))


def halves(x):
    high = x.astype(BF16)
    return high, (x - high.astype(F32)).astype(BF16)


def dot(a, b):
    return jnp.dot(a, b, preferred_element_type=F32)


def dot_const_left(const, x):
    high, low = halves(x)
    return dot(const[0], high) + dot(const[0], low) + dot(const[1], high)


def dot_const_right(x, const):
    high, low = halves(x)
    return dot(high, const[0]) + dot(low, const[0]) + dot(high, const[1])


def forward(signals, outer, inner, turns):
    groups = [x[:, 8 * i : 8 * i + 8, :].reshape(256, 128) for x in signals for i in range(2)]
    y = dot_const_left(outer, jnp.concatenate(groups, axis=1))
    cos, sin = turns[0], turns[1]
    rest = jnp.zeros((8, 128), F32)
    rows = []
    for i in range(len(groups)):
        part = y[:, 128 * i : 128 * i + 128]
        re, im = part[:264], jnp.concatenate([rest, part[264:], rest], axis=0)
        rows.append(jnp.concatenate([re * cos + im * sin, im * cos - re * sin], axis=1))
    z = dot_const_right(jnp.concatenate(rows, axis=0), inner)
    return [(z[528 * i : 528 * i + 528, :128], z[528 * i : 528 * i + 528, 128:]) for i in range(len(signals))]


def inverse(spectra, outer_back, inner_back, turns):
    z = jnp.concatenate([jnp.concatenate(pair, axis=1) for pair in spectra], axis=0)
    z = dot_const_right(z, inner_back)
    cos, sin = turns[0], turns[1]
    columns = []
    for i in range(2 * len(spectra)):
        re, im = z[264 * i : 264 * i + 264, :128], z[264 * i : 264 * i + 264, 128:]
        columns.append(jnp.concatenate([re * cos - im * sin, (im * cos + re * sin)[8:256]], axis=0))
    y = dot_const_left(outer_back, jnp.concatenate(columns, axis=1))
    groups = [y[:, 128 * i : 128 * i + 128].reshape(PARTS, 8, 128) for i in range(len(columns))]
    return [jnp.concatenate(groups[2 * i : 2 * i + 2], axis=1) for i in range(len(spectra))]


def pack(x, scale):
    x = x * scale
    square = x * x
    return (square * (x * jnp.abs(x))).astype(BF16)


def unpack(code, scale):
    code = code.astype(F32)
    size = jnp.sqrt(jnp.sqrt(jnp.abs(code))) * (1.0 / scale)
    return jnp.where(code < 0.0, -size, size)


class Wire:
    def __init__(self, send, recv):
        self.send, self.recv, self.made = send, recv, []

    def go(self, src, dst, to, there=None):
        i = len(self.made)
        copy = pltpu.make_async_remote_copy(
            src_ref=src,
            dst_ref=dst,
            send_sem=self.send.at[i],
            recv_sem=self.recv.at[i if there is None else there],
            device_id=to,
            device_id_type=MESH,
        )
        copy.start()
        self.made.append(copy)
        return copy

    def drain(self):
        for copy in self.made:
            copy.wait_send()


def place(x, z, k):
    return x * 16 + lax.rem(z + NZ, NZ) * 2 + k


def gather_seq(wire, buf, x, z, k):
    rows = buf.shape[1]
    half, quarter = rows // 2, rows // 4
    low, high, full = (0, half), (half, half), (0, rows)

    def send(src_x, src_z, part, dst):
        ref = buf.at[place(src_x, src_z, k), pl.ds(*part)]
        return wire.go(ref, ref, {"seq": place(*dst)})

    sib, par, right, left = (x, z, 1 - k), (1 - x, z, k), (x, z + 1, k), (x, z - 1, k)
    other = 1 - x
    siblings, across = [], []
    r = send(x, z, full, right)
    l = send(x, z, full, left)
    first = send(x, z, full, par)
    siblings.append(send(x, z, full, sib))
    yield
    first.wait_recv()
    pr = send(other, z, low, right)
    pl_ = send(other, z, low, left)
    siblings.append(send(other, z, full, sib))
    yield
    for j in (1, 2, 3):
        r.wait_recv()
        r = send(x, z - j, full if j < 3 else low, right)
        across.append((z - j, send(x, z - j, high, par)))
        siblings.append(send(x, z - j, full, sib))
        l.wait_recv()
        l = send(x, z + j, full if j < 3 else high, left)
        across.append((z + j, send(x, z + j, high, par)))
        siblings.append(send(x, z + j, full, sib))
        pr.wait_recv()
        pr = send(other, z - j, low if j < 3 else (0, quarter), right)
        siblings.append(send(other, z - j, low, sib))
        pl_.wait_recv()
        pl_ = send(other, z + j, low if j < 3 else (quarter, quarter), left)
        siblings.append(send(other, z + j, low, sib))
        yield
    l.wait_recv()
    across.append((z + 4, send(x, z + 4, high, par)))
    siblings.append(send(x, z + 4, high, sib))
    r.wait_recv()
    siblings.append(send(x, z + 4, low, sib))
    pr.wait_recv()
    pl_.wait_recv()
    siblings.append(send(other, z + 4, low, sib))
    yield
    for far, copy in across:
        copy.wait_recv()
        siblings.append(send(other, far, high, sib))
    yield
    for copy in siblings:
        copy.wait_recv()
    yield


def ring_z(wire, buf, x, z, k):
    half = buf.shape[1] // 2
    low, high, full = (0, half), (half, half), (0, 2 * half)

    def ref(far, part):
        return buf.at[lax.rem(z + far + NZ, NZ) * 2 + k, pl.ds(*part)]

    def send(far, part, step):
        r = ref(far, part)
        return wire.go(r, r, {"seq": place(x, z + step, k)})

    def share(far):
        r = ref(far, full)
        return wire.go(r, r, {"seq": place(x, z, 1 - k)})

    right, left = send(0, low, 1), send(0, high, -1)
    right2, left2 = send(0, high, 1), send(0, low, -1)
    siblings = [share(0)]
    yield
    for j in (1, 2, 3):
        right.wait_recv()
        right = send(-j, low, 1)
        left.wait_recv()
        left = send(j, high, -1)
        right2.wait_recv()
        right2 = send(-j, high, 1) if j < 3 else None
        left2.wait_recv()
        left2 = send(j, low, -1) if j < 3 else None
        siblings += [share(-j), share(j)]
        yield
    right.wait_recv()
    left.wait_recv()
    siblings.append(share(4))
    yield
    for copy in siblings:
        copy.wait_recv()
    yield


def gather_ch(wire, buf, y, x):
    half = buf.shape[1] // 2

    def send(src_y, src_x, part, dst_y, dst_x):
        ref = buf.at[lax.rem(src_y + NY, NY) * 2 + src_x, pl.ds(*part)]
        return wire.go(ref, ref, {"ch": lax.rem(dst_y + NY, NY) * 2 + dst_x})

    full, low, high = (0, 2 * half), (0, half), (half, half)
    first = send(y, x, full, y, 1 - x)
    near = [send(y, x, full, y + 1, x), send(y, x, full, y - 1, x)]
    yield
    first.wait_recv()
    near += [send(y, 1 - x, full, y + 1, x), send(y, 1 - x, full, y - 1, x)]
    yield
    far = []
    for i, copy in enumerate(near):
        copy.wait_recv()
        whose = x if i < 2 else 1 - x
        if i % 2 == 0:
            far.append(send(y - 1, whose, low, y + 1, x))
        else:
            far.append(send(y + 1, whose, high, y - 1, x))
    yield
    for copy in far:
        copy.wait_recv()
    yield


def advance(steps, count=1):
    for _ in range(count):
        next(steps, None)


def finish(steps):
    for _ in steps:
        pass


class Swap:
    def __init__(self, src, dst, send, recv, me):
        self.src, self.dst, self.send, self.recv, self.me = src, dst, send, recv, me

    def copy(self, d):
        target = lax.rem(self.me + d, PARTS)
        return pltpu.make_async_remote_copy(
            src_ref=self.src.at[target],
            dst_ref=self.dst.at[self.me],
            send_sem=self.send.at[d],
            recv_sem=self.recv.at[d],
            device_id={"seq": target},
            device_id_type=MESH,
        )

    def start(self, low=1, high=PARTS):
        @pl.loop(low, high)
        def _(d):
            self.copy(d).start()

        if low == 1:
            self.dst[self.me] = self.src[self.me]

    def wait(self):
        @pl.loop(1, PARTS)
        def _(d):
            self.copy(d).wait()


def envelope_of(rates, me, rows):
    total = rows * PARTS
    spot = me * rows + lax.broadcasted_iota(jnp.int32, (rows, 1), 0)
    spot = spot.astype(F32) / total
    scaling = jnp.sqrt(2.0 * rates / (total * (1.0 - jnp.exp(-2.0 * rates))))
    return jnp.exp(-spot * rates) * scaling


def whole(
    q_hbm, k_hbm, v_hbm, f_hbm, r_hbm, w_hbm, c_hbm,
    outer_hbm, outer_back_hbm, inner_hbm, inner_back_hbm, turns_hbm,
    gq_hbm, gk_hbm, gv_hbm, gf_hbm, gw_hbm,
    q_ref, k_ref, v_ref, f_ref, r_ref, outer_ref, outer_back_ref, inner_ref, inner_back_ref, turns,
    gq_out, gk_out, gv_out, gf_out, gw_out, outer, outer_back, inner, inner_back,
    wbuf, cbuf, tall, gbuf, rate_ref,
    in_src, in_dst, gm_src, gm_dst, home_src, home_dst, qt_ref, half_src, half_dst,
    load_sem, store_sem, wire_send, wire_recv, swap_send, swap_recv,
):
    me, ch = lax.axis_index("seq"), lax.axis_index("ch")
    x, z, k = me // 16, lax.rem(me // 2, NZ), lax.rem(me, 2)
    zk = lax.rem(me, 16)
    y, xl = ch // 2, lax.rem(ch, 2)
    rows, chans = q_ref.shape
    fine = chans // PARTS
    wire = Wire(wire_send, wire_recv)

    loads = [
        pltpu.make_async_copy(src, dst, load_sem.at[i])
        for i, (src, dst) in enumerate(
            (
                (w_hbm, wbuf.at[me]),
                (c_hbm, cbuf.at[ch]),
                (k_hbm, k_ref),
                (v_hbm, v_ref),
                (f_hbm, f_ref),
                (q_hbm, q_ref),
                (r_hbm, r_ref),
                (outer_hbm, outer_ref),
                (outer_back_hbm, outer_back_ref),
                (inner_hbm, inner_ref),
                (inner_back_hbm, inner_back_ref),
                (turns_hbm, turns),
            )
        )
    ]
    for load in loads:
        load.start()

    spot = (ch // 4) * 16 + zk
    keeper = lax.rem(spot // 4 + 1 + lax.rem(spot, 4), WIDE)
    targets = [{"seq": x * 16 + lax.rem(ch, 4) * 4 + i, "ch": keeper} for i in range(4)]
    sources = []
    for j in range(4):
        theirs = 4 * lax.rem(ch - 1 - j + WIDE, WIDE) + j
        sources.append(
            {"seq": x * 16 + lax.rem(theirs, 16), "ch": (theirs // 16) * 4 + zk // 4}
        )
    around = [
        {"ch": y * 2 + 1 - xl},
        {"ch": lax.rem(y + 1, NY) * 2 + xl},
        {"ch": lax.rem(y + NY - 1, NY) * 2 + xl},
    ]
    greeted = targets + sources + around
    barrier = pltpu.get_barrier_semaphore()

    @pl.loop(1, PARTS)
    def _(d):
        pl.semaphore_signal(
            barrier, inc=1, device_id={"seq": lax.rem(me + d, PARTS)}, device_id_type=MESH
        )

    for to in greeted:
        pl.semaphore_signal(barrier, inc=1, device_id=to, device_id_type=MESH)

    for load in loads:
        load.wait()

    def turned(value):
        return value.T.reshape(PARTS, fine, rows)

    in_src[:, 0:16] = pack(turned(k_ref[...].astype(F32) * v_ref[...].astype(F32)), 2.0**25)
    in_src[:, 16:32] = pack(turned(f_ref[...]), 2.0**28)
    qt_ref[...] = q_ref[...].astype(F32).T
    for wide_const, const in (
        (outer_ref, outer), (outer_back_ref, outer_back), (inner_ref, inner), (inner_back_ref, inner_back)
    ):
        const[0], const[1] = halves(wide_const[...])
    rate_ref[...] = jnp.broadcast_to(r_ref[...], (rows, chans)).T
    env = envelope_of(r_ref[...], me, rows)
    own_rates = rate_ref[pl.ds(me * fine, fine), :]
    lanes = lax.broadcasted_iota(jnp.int32, (fine, rows), 1)
    span = float(rows * PARTS)
    own_scaling = jnp.sqrt(2.0 * own_rates / (span * (1.0 - jnp.exp(-2.0 * own_rates))))
    envelope = jnp.stack(
        [
            jnp.exp(-((lanes + block * rows).astype(F32) / span) * own_rates) * own_scaling
            for block in range(PARTS)
        ]
    )
    pl.semaphore_wait(barrier, PARTS - 1 + len(greeted))

    weights = gather_seq(wire, wbuf, x, z, k)
    advance(weights)
    wide = gather_ch(wire, cbuf, y, xl)
    advance(wide)
    def swap(i, src, dst):
        return Swap(src, dst, swap_send.at[i], swap_recv.at[i], me)

    stores = []

    def store(src, dst):
        copy = pltpu.make_async_copy(src, dst, store_sem.at[len(stores)])
        copy.start()
        stores.append(copy)

    early = swap(0, in_src, in_dst)
    late = swap(1, gm_src, gm_dst)
    homes = [swap(2 + i, home_src.at[i], home_dst.at[i]) for i in range(3)]

    early.start()
    advance(weights, 2)
    advance(wide)
    advance(weights)
    advance(wide)
    base = len(wire.made)
    for i, to in enumerate(targets):
        src = cbuf.at[ch, :, pl.ds(i * 128, 128)]
        wire.go(src, tall.at[keeper, lax.rem(me, 4)], to, base + lax.rem(me, 4))
    early.wait()
    product = unpack(in_dst[:, 0:16], 2.0**25)
    filt = unpack(in_dst[:, 16:32], 2.0**28) * envelope
    (pr, pi), (fr, fi) = forward([product, filt], outer, inner, turns)
    advance(weights)
    (mixed,) = inverse([(pr * fr - pi * fi, pr * fi + pi * fr)], outer_back, inner_back, turns)
    home_src[0] = pack(mixed, 2.0**17)
    homes[0].start()
    advance(weights)
    finish(wide)
    finish(weights)

    homes[0].wait()
    mixed_home = unpack(home_dst[0].reshape(chans, rows), 2.0**17)
    gbuf[zk] = (qt_ref[...] * mixed_home).astype(BF16)
    ring = ring_z(wire, gbuf, x, z, k)
    advance(ring)
    for j in range(4):
        pltpu.make_async_copy(tall.at[0, 0], tall.at[0, 0], wire_recv.at[base + j]).wait()
    high = gather_ch(wire, tall, y, xl)
    advance(high)
    total = jnp.zeros((rows, chans), F32)
    for h in range(WIDE):
        part = jnp.concatenate([wbuf[4 * h + i] for i in range(4)], axis=1)
        total += lax.dot_general(
            cbuf[h], part, (((1,), (1,)), ((), ())), preferred_element_type=F32
        )
    gm_src[...] = pack(turned(q_ref[...].astype(F32) * total), 2.0**17)
    late.start()
    advance(ring)
    advance(high)
    gq_out[...] = (mixed_home.T * total).astype(BF16)
    store(gq_out, gq_hbm)
    advance(ring)
    advance(high)
    late.wait()
    grad = unpack(gm_dst[...], 2.0**17)
    ((gr, gi),) = forward([grad], outer, inner, turns)
    advance(ring)
    back_product, back_taps = inverse(
        [(gr * fr + gi * fi, gi * fr - gr * fi), (gr * pr + gi * pi, gi * pr - gr * pi)],
        outer_back, inner_back, turns,
    )
    home_src[1] = pack(back_product, 2.0**8)
    homes[1].start()
    home_src[2] = pack(back_taps, 1.0)
    homes[2].start()
    finish(ring)
    finish(high)

    total = jnp.zeros((chans, 256), F32)
    for a in range(4):
        left = [gbuf[4 * a + j] for j in range(4)]
        right = [
            jnp.concatenate([tall[(4 * i + a + 1 + j) % WIDE, j] for i in range(2)], axis=1)
            for j in range(4)
        ]
        total += dot(jnp.concatenate(left, axis=1), jnp.concatenate(right, axis=0))
    mine = jnp.where(x == 0, total[:, :128], total[:, 128:])
    theirs = jnp.where(x == 0, total[:, 128:], total[:, :128])
    half_src[...] = pack(theirs, 1.0)
    last = wire.go(half_src, half_dst, {"seq": place(1 - x, z, k)})

    def arrived(i, scale):
        homes[i].wait()
        return unpack(home_dst[i].reshape(chans, rows), scale).T

    grad_product = arrived(1, 2.0**8)
    gk_out[...] = (grad_product * v_ref[...].astype(F32)).astype(BF16)
    store(gk_out, gk_hbm)
    gv_out[...] = (grad_product * k_ref[...].astype(F32)).astype(BF16)
    store(gv_out, gv_hbm)
    gf_out[...] = arrived(2, 1.0) * env
    store(gf_out, gf_hbm)
    last.wait_recv()
    gw_out[...] = mine + unpack(half_dst[...], 1.0)
    store(gw_out, gw_hbm)
    for copy in stores:
        copy.wait()
    wire.drain()


def hand_over(*refs):
    src, dst, held, load_sem, store_sem = refs[:5], refs[5:10], refs[10:15], refs[15], refs[16]
    loads = [pltpu.make_async_copy(src[i], held[i], load_sem.at[i]) for i in range(5)]
    stores = [pltpu.make_async_copy(held[i], dst[i], store_sem.at[i]) for i in range(5)]
    for load in loads:
        load.start()
    for load, copy in zip(loads, stores):
        load.wait()
        copy.start()
    for copy in stores:
        copy.wait()


def on_device(query, key, value, filter_raw, rates, out_weight, cotangent):
    rows, chans = query.shape
    fine = chans // PARTS
    tables = transform_tables(rows)
    columns = out_weight.shape[1]
    shape = jax.ShapeDtypeStruct
    block = pltpu.VMEM((rows, chans), BF16)
    piece = (PARTS, fine, rows)
    out_shape = (
        shape((rows, chans), BF16),
        shape((rows, chans), BF16),
        shape((rows, chans), BF16),
        shape((rows, chans), F32),
        shape(out_weight.shape, F32),
    )
    anywhere = pl.BlockSpec(memory_space=pl.ANY)
    results = pl.pallas_call(
        whole,
        out_shape=out_shape,
        in_specs=[anywhere] * 12,
        out_specs=(anywhere,) * 5,
        scratch_shapes=[
            block,
            block,
            block,
            pltpu.VMEM((rows, chans), F32),
            pltpu.VMEM((1, chans), F32),
            *(pltpu.VMEM(t.shape, t.dtype) for t in tables),
            *(pltpu.VMEM(o.shape, o.dtype) for o in out_shape),
            *(pltpu.VMEM((2, *t.shape), BF16) for t in tables[:4]),
            pltpu.VMEM((PARTS, chans, columns), BF16),
            pltpu.VMEM((WIDE, rows, chans), BF16),
            pltpu.VMEM((WIDE, 4, rows, columns), BF16),
            pltpu.VMEM((16, chans, rows), BF16),
            pltpu.VMEM((chans, rows), F32),
            pltpu.VMEM((PARTS, 2 * fine, rows), BF16),
            pltpu.VMEM((PARTS, 2 * fine, rows), BF16),
            pltpu.VMEM(piece, BF16),
            pltpu.VMEM(piece, BF16),
            pltpu.VMEM((3, *piece), BF16),
            pltpu.VMEM((3, *piece), BF16),
            pltpu.VMEM((chans, rows), F32),
            pltpu.VMEM((chans, columns), BF16),
            pltpu.VMEM((chans, columns), BF16),
            pltpu.SemaphoreType.DMA((12,)),
            pltpu.SemaphoreType.DMA((5,)),
            pltpu.SemaphoreType.DMA((128,)),
            pltpu.SemaphoreType.DMA((128,)),
            pltpu.SemaphoreType.DMA((5, PARTS)),
            pltpu.SemaphoreType.DMA((5, PARTS)),
        ],
        compiler_params=pltpu.CompilerParams(
            collective_id=0, has_side_effects=True, vmem_limit_bytes=63 * 2**20
        ),
        name="whole",
    )(
        query, key, value, filter_raw, rates.reshape(1, chans), out_weight, cotangent,
        *(jnp.asarray(t) for t in tables),
    )
    return pl.pallas_call(
        hand_over,
        out_shape=out_shape,
        in_specs=[anywhere] * 5,
        out_specs=(anywhere,) * 5,
        scratch_shapes=[pltpu.VMEM(o.shape, o.dtype) for o in out_shape]
        + [pltpu.SemaphoreType.DMA((5,)), pltpu.SemaphoreType.DMA((5,))],
        compiler_params=pltpu.CompilerParams(vmem_limit_bytes=63 * 2**20),
        name="hand_over",
    )(*results)


def solution(mesh):
    return jax.shard_map(
        on_device,
        mesh=mesh,
        in_specs=(
            P("seq", "ch"),
            P("seq", "ch"),
            P("seq", "ch"),
            P("seq", "ch"),
            P("ch"),
            P("ch", "seq"),
            P("seq", "ch"),
        ),
        out_specs=(P("seq", "ch"), P("seq", "ch"), P("seq", "ch"), P("seq", "ch"), P("ch", "seq")),
        check_vma=False,
    )
```

```python
import math

import jax
import jax.numpy as jnp
import numpy as np
from jax import lax
from jax.experimental import pallas as pl
from jax.experimental.pallas import tpu as pltpu
from jax.sharding import PartitionSpec as P

MESH = pl.DeviceIdType.MESH
F32 = jnp.float32
BF16 = jnp.bfloat16
NZ, NY, PARTS, WIDE = 8, 4, 32, 8


def transform_tables(rows):
    total = 2 * PARTS * rows
    k1 = np.arange(PARTS + 1)[:, None]
    n1 = np.arange(PARTS)[None, :]
    turn = 2 * math.pi * ((k1 * n1) % (2 * PARTS)) / (2 * PARTS)
    eye = np.eye(8)
    outer = np.kron(np.concatenate([np.cos(turn), -np.sin(turn)[1:-1]], 0), eye)
    weight = np.full((PARTS + 1, 1), 2.0)
    weight[0] = weight[-1] = 1.0
    outer_back = np.concatenate([weight * np.cos(turn), (-weight * np.sin(turn))[1:-1]], 0)
    outer_back = np.kron(outer_back.T / total, eye)
    n2 = np.arange(rows)
    twist = np.repeat(2 * math.pi * (k1 * n2[None, :]) / total, 8, axis=0)
    inner = 2 * math.pi * ((n2[:, None] * n2[None, :]) % rows) / rows
    cos, sin = np.cos(inner), np.sin(inner)
    ahead = np.block([[cos, -sin], [sin, cos]])
    back = np.block([[cos, sin], [-sin, cos]])

    turns = np.stack([np.cos(twist), np.sin(twist)])
    return tuple(np.asarray(m, np.float32) for m in (outer, outer_back, ahead, back, turns))


def halves(x):
    high = x.astype(BF16)
    return high, (x - high.astype(F32)).astype(BF16)


def dot(a, b):
    return jnp.dot(a, b, preferred_element_type=F32)


def dot_const_left(const, x):
    high, low = halves(x)
    return dot(const[0], high) + dot(const[0], low) + dot(const[1], high)


def dot_const_right(x, const):
    high, low = halves(x)
    return dot(high, const[0]) + dot(low, const[0]) + dot(high, const[1])


def forward(signals, outer, inner, turns):
    groups = [x[:, 8 * i : 8 * i + 8, :].reshape(256, 128) for x in signals for i in range(2)]
    y = dot_const_left(outer, jnp.concatenate(groups, axis=1))
    cos, sin = turns[0], turns[1]
    rest = jnp.zeros((8, 128), F32)
    rows = []
    for i in range(len(groups)):
        part = y[:, 128 * i : 128 * i + 128]
        re, im = part[:264], jnp.concatenate([rest, part[264:], rest], axis=0)
        rows.append(jnp.concatenate([re * cos + im * sin, im * cos - re * sin], axis=1))
    z = dot_const_right(jnp.concatenate(rows, axis=0), inner)
    return [(z[528 * i : 528 * i + 528, :128], z[528 * i : 528 * i + 528, 128:]) for i in range(len(signals))]


def inverse(spectra, outer_back, inner_back, turns):
    z = jnp.concatenate([jnp.concatenate(pair, axis=1) for pair in spectra], axis=0)
    z = dot_const_right(z, inner_back)
    cos, sin = turns[0], turns[1]
    columns = []
    for i in range(2 * len(spectra)):
        re, im = z[264 * i : 264 * i + 264, :128], z[264 * i : 264 * i + 264, 128:]
        columns.append(jnp.concatenate([re * cos - im * sin, (im * cos + re * sin)[8:256]], axis=0))
    y = dot_const_left(outer_back, jnp.concatenate(columns, axis=1))
    groups = [y[:, 128 * i : 128 * i + 128].reshape(PARTS, 8, 128) for i in range(len(columns))]
    return [jnp.concatenate(groups[2 * i : 2 * i + 2], axis=1) for i in range(len(spectra))]


def pack(x, scale):
    x = x * scale
    square = x * x
    return (square * (x * jnp.abs(x))).astype(BF16)


def unpack(code, scale):
    code = code.astype(F32)
    size = jnp.sqrt(jnp.sqrt(jnp.abs(code))) * (1.0 / scale)
    return jnp.where(code < 0.0, -size, size)


class Wire:
    def __init__(self, send, recv):
        self.send, self.recv, self.made = send, recv, []

    def go(self, src, dst, to, there=None):
        i = len(self.made)
        copy = pltpu.make_async_remote_copy(
            src_ref=src,
            dst_ref=dst,
            send_sem=self.send.at[i],
            recv_sem=self.recv.at[i if there is None else there],
            device_id=to,
            device_id_type=MESH,
        )
        copy.start()
        self.made.append(copy)
        return copy

    def drain(self):
        for copy in self.made:
            copy.wait_send()


def place(x, z, k):
    return x * 16 + lax.rem(z + NZ, NZ) * 2 + k


def gather_seq(wire, buf, x, z, k):
    rows = buf.shape[1]
    cut = rows * 4 // 8
    low, high, full = (0, cut), (cut, rows - cut), (0, rows)

    def send(src_x, src_z, part, dst):
        ref = buf.at[place(src_x, src_z, k), pl.ds(*part)]
        return wire.go(ref, ref, {"seq": place(*dst)})

    sib, par, right, left = (x, z, 1 - k), (1 - x, z, k), (x, z + 1, k), (x, z - 1, k)
    other = 1 - x
    right_high, left_high = send(x, z, high, right), send(x, z, high, left)
    first = send(x, z, low, par)
    right_low, left_low = send(x, z, low, right), send(x, z, low, left)
    across = [(z, send(x, z, high, par))]
    siblings = [send(x, z, full, sib)]
    yield
    first.wait_recv()
    right_other, left_other = send(other, z, low, right), send(other, z, low, left)
    yield
    for j in (1, 2, 3):
        right_high.wait_recv()
        right_high = send(x, z - j, high, right) if j < 3 else None
        behind = send(x, z - j, high, par)
        left_high.wait_recv()
        left_high = send(x, z + j, high, left)
        ahead = send(x, z + j, high, par)
        right_low.wait_recv()
        right_low = send(x, z - j, low, right)
        siblings.append(send(x, z - j, full, sib))
        left_low.wait_recv()
        left_low = send(x, z + j, low, left) if j < 3 else None
        siblings.append(send(x, z + j, full, sib))
        right_other.wait_recv()
        right_other = send(other, z - j, low if j < 3 else (0, cut // 2), right)
        left_other.wait_recv()
        left_other = send(other, z + j, low if j < 3 else (cut // 2, cut // 2), left)
        for far, copy in across:
            copy.wait_recv()
            siblings.append(send(other, far, full, sib))
        across = [(z - j, behind), (z + j, ahead)]
        yield
    left_high.wait_recv()
    last = send(x, z + 4, high, par)
    siblings.append(send(x, z + 4, high, sib))
    right_low.wait_recv()
    siblings.append(send(x, z + 4, low, sib))
    for far, copy in across:
        copy.wait_recv()
        siblings.append(send(other, far, full, sib))
    right_other.wait_recv()
    left_other.wait_recv()
    siblings.append(send(other, z + 4, low, sib))
    yield
    last.wait_recv()
    siblings.append(send(other, z + 4, high, sib))
    yield
    for copy in siblings:
        copy.wait_recv()
    yield


def ring_z(wire, buf, x, z, k):
    half = buf.shape[1] // 2
    low, high, full = (0, half), (half, half), (0, 2 * half)

    def ref(far, part):
        return buf.at[lax.rem(z + far + NZ, NZ) * 2 + k, pl.ds(*part)]

    def send(far, part, step):
        r = ref(far, part)
        return wire.go(r, r, {"seq": place(x, z + step, k)})

    def share(far):
        r = ref(far, full)
        return wire.go(r, r, {"seq": place(x, z, 1 - k)})

    right, left = send(0, low, 1), send(0, high, -1)
    right2, left2 = send(0, high, 1), send(0, low, -1)
    siblings = [share(0)]
    yield
    for j in (1, 2, 3):
        right.wait_recv()
        right = send(-j, low, 1)
        left.wait_recv()
        left = send(j, high, -1)
        right2.wait_recv()
        right2 = send(-j, high, 1) if j < 3 else None
        left2.wait_recv()
        left2 = send(j, low, -1) if j < 3 else None
        siblings += [share(-j), share(j)]
        yield
    right.wait_recv()
    left.wait_recv()
    siblings.append(share(4))
    yield
    for copy in siblings:
        copy.wait_recv()
    yield


def gather_ch(wire, buf, y, x):
    half = buf.shape[1] // 2

    def send(src_y, src_x, part, dst_y, dst_x):
        ref = buf.at[lax.rem(src_y + NY, NY) * 2 + src_x, pl.ds(*part)]
        return wire.go(ref, ref, {"ch": lax.rem(dst_y + NY, NY) * 2 + dst_x})

    full, low, high = (0, 2 * half), (0, half), (half, half)
    first = send(y, x, full, y, 1 - x)
    near = [send(y, x, full, y + 1, x), send(y, x, full, y - 1, x)]
    yield
    first.wait_recv()
    near += [send(y, 1 - x, full, y + 1, x), send(y, 1 - x, full, y - 1, x)]
    yield
    far = []
    for i, copy in enumerate(near):
        copy.wait_recv()
        whose = x if i < 2 else 1 - x
        if i % 2 == 0:
            far.append(send(y - 1, whose, low, y + 1, x))
        else:
            far.append(send(y + 1, whose, high, y - 1, x))
    yield
    for copy in far:
        copy.wait_recv()
    yield


def advance(steps, count=1):
    for _ in range(count):
        next(steps, None)


def finish(steps):
    for _ in steps:
        pass


class Swap:
    def __init__(self, src, dst, send, recv, me):
        self.src, self.dst, self.send, self.recv, self.me = src, dst, send, recv, me

    def copy(self, d):
        target = lax.rem(self.me + d, PARTS)
        return pltpu.make_async_remote_copy(
            src_ref=self.src.at[target],
            dst_ref=self.dst.at[self.me],
            send_sem=self.send,
            recv_sem=self.recv,
            device_id={"seq": target},
            device_id_type=MESH,
        )

    def start(self, low=1, high=PARTS):
        @pl.loop(low, high)
        def _(d):
            self.copy(d).start()

        if low == 1:
            self.dst[self.me] = self.src[self.me]

    def wait(self):
        for ref, sem in ((self.dst, self.recv), (self.src, self.send)):
            all_pieces = ref.at[pl.ds(0, PARTS - 1)]
            pltpu.make_async_copy(all_pieces, all_pieces, sem).wait()


def envelope_of(rates, me, rows):
    total = rows * PARTS
    spot = me * rows + lax.broadcasted_iota(jnp.int32, (rows, 1), 0)
    spot = spot.astype(F32) / total
    scaling = jnp.sqrt(2.0 * rates / (total * (1.0 - jnp.exp(-2.0 * rates))))
    return jnp.exp(-spot * rates) * scaling


def whole(
    q_hbm, k_hbm, v_hbm, f_hbm, r_hbm, w_hbm, c_hbm,
    outer_hbm, outer_back_hbm, inner_hbm, inner_back_hbm, turns_hbm,
    gq_hbm, gk_hbm, gv_hbm, gf_hbm, gw_hbm,
    q_ref, k_ref, v_ref, f_ref, r_ref, outer_ref, outer_back_ref, inner_ref, inner_back_ref, turns,
    gq_out, gk_out, gv_out, gf_out, gw_out, outer, outer_back, inner, inner_back,
    wbuf, cbuf, tall, gbuf, rate_ref,
    in_src, in_dst, gm_src, gm_dst, home_src, home_dst, qt_ref, half_src, half_dst,
    load_sem, store_sem, wire_send, wire_recv, swap_send, swap_recv,
):
    me, ch = lax.axis_index("seq"), lax.axis_index("ch")
    x, z, k = me // 16, lax.rem(me // 2, NZ), lax.rem(me, 2)
    zk = lax.rem(me, 16)
    y, xl = ch // 2, lax.rem(ch, 2)
    rows, chans = q_ref.shape
    fine = chans // PARTS
    wire = Wire(wire_send, wire_recv)

    loads = [
        pltpu.make_async_copy(src, dst, load_sem.at[i])
        for i, (src, dst) in enumerate(
            (
                (w_hbm, wbuf.at[me]),
                (c_hbm, cbuf.at[ch]),
                (k_hbm, k_ref),
                (v_hbm, v_ref),
                (f_hbm, f_ref),
                (q_hbm, q_ref),
                (r_hbm, r_ref),
                (outer_hbm, outer_ref),
                (outer_back_hbm, outer_back_ref),
                (inner_hbm, inner_ref),
                (inner_back_hbm, inner_back_ref),
                (turns_hbm, turns),
            )
        )
    ]
    for load in loads:
        load.start()

    spot = (ch // 4) * 16 + zk
    keeper = lax.rem(spot // 4 + 1 + lax.rem(spot, 4), WIDE)
    targets = [{"seq": x * 16 + lax.rem(ch, 4) * 4 + i, "ch": keeper} for i in range(4)]
    sources = []
    for j in range(4):
        theirs = 4 * lax.rem(ch - 1 - j + WIDE, WIDE) + j
        sources.append(
            {"seq": x * 16 + lax.rem(theirs, 16), "ch": (theirs // 16) * 4 + zk // 4}
        )
    around = [
        {"ch": y * 2 + 1 - xl},
        {"ch": lax.rem(y + 1, NY) * 2 + xl},
        {"ch": lax.rem(y + NY - 1, NY) * 2 + xl},
    ]
    greeted = targets + sources + around
    barrier = pltpu.get_barrier_semaphore()

    @pl.loop(1, PARTS)
    def _(d):
        pl.semaphore_signal(
            barrier, inc=1, device_id={"seq": lax.rem(me + d, PARTS)}, device_id_type=MESH
        )

    for to in greeted:
        pl.semaphore_signal(barrier, inc=1, device_id=to, device_id_type=MESH)


    def turned(value):
        return value.T.reshape(PARTS, fine, rows)

    def swap(i, src, dst):
        return Swap(src, dst, swap_send.at[i], swap_recv.at[i], me)

    stores = []

    def store(src, dst):
        copy = pltpu.make_async_copy(src, dst, store_sem.at[len(stores)])
        copy.start()
        stores.append(copy)

    early = swap(0, in_src, in_dst)
    late = swap(1, gm_src, gm_dst)
    homes = [swap(2 + i, home_src.at[i], home_dst.at[i]) for i in range(3)]

    loads[0].wait()
    loads[1].wait()
    pl.semaphore_wait(barrier, PARTS - 1 + len(greeted))
    weights = gather_seq(wire, wbuf, x, z, k)
    advance(weights)
    wide = gather_ch(wire, cbuf, y, xl)
    advance(wide)
    for load in loads[2:5]:
        load.wait()
    in_src[:, 0:16] = pack(turned(k_ref[...].astype(F32) * v_ref[...].astype(F32)), 2.0**25)
    in_src[:, 16:32] = pack(turned(f_ref[...]), 2.0**28)
    early.start()
    advance(weights)
    advance(wide)
    for load in loads[5:]:
        load.wait()
    qt_ref[...] = q_ref[...].astype(F32).T
    for wide_const, const in (
        (outer_ref, outer), (outer_back_ref, outer_back), (inner_ref, inner), (inner_back_ref, inner_back)
    ):
        const[0], const[1] = halves(wide_const[...])
    rate_ref[...] = jnp.broadcast_to(r_ref[...], (rows, chans)).T
    env = envelope_of(r_ref[...], me, rows)
    own_rates = rate_ref[pl.ds(me * fine, fine), :]
    lanes = lax.broadcasted_iota(jnp.int32, (fine, rows), 1)
    span = float(rows * PARTS)
    own_scaling = jnp.sqrt(2.0 * own_rates / (span * (1.0 - jnp.exp(-2.0 * own_rates))))
    envelope = jnp.stack(
        [
            jnp.exp(-((lanes + block * rows).astype(F32) / span) * own_rates) * own_scaling
            for block in range(PARTS)
        ]
    )
    advance(weights)
    advance(weights)
    early.wait()
    product = unpack(in_dst[:, 0:16], 2.0**25)
    filt = unpack(in_dst[:, 16:32], 2.0**28) * envelope
    (pr, pi), (fr, fi) = forward([product, filt], outer, inner, turns)
    advance(weights)
    advance(wide)
    (mixed,) = inverse([(pr * fr - pi * fi, pr * fi + pi * fr)], outer_back, inner_back, turns)
    home_src[0] = pack(mixed, 2.0**17)
    homes[0].start()
    base = len(wire.made)
    for i, to in enumerate(targets):
        src = cbuf.at[ch, :, pl.ds(i * 128, 128)]
        wire.go(src, tall.at[keeper, lax.rem(me, 4)], to, base + lax.rem(me, 4))
    advance(weights)
    finish(wide)
    advance(weights)
    homes[0].wait()
    mixed_home = unpack(home_dst[0].reshape(chans, rows), 2.0**17)
    gbuf[zk] = (qt_ref[...] * mixed_home).astype(BF16)
    ring = ring_z(wire, gbuf, x, z, k)
    advance(ring)
    finish(weights)
    for j in range(4):
        pltpu.make_async_copy(tall.at[0, 0], tall.at[0, 0], wire_recv.at[base + j]).wait()
    high = gather_ch(wire, tall, y, xl)
    advance(high)
    total = jnp.zeros((rows, chans), F32)
    for h in range(WIDE):
        part = jnp.concatenate([wbuf[4 * h + i] for i in range(4)], axis=1)
        total += lax.dot_general(
            cbuf[h], part, (((1,), (1,)), ((), ())), preferred_element_type=F32
        )
    gm_src[...] = pack(turned(q_ref[...].astype(F32) * total), 2.0**17)
    late.start()
    advance(ring)
    advance(high)
    gq_out[...] = (mixed_home.T * total).astype(BF16)
    store(gq_out, gq_hbm)
    advance(ring)
    advance(high)
    late.wait()
    grad = unpack(gm_dst[...], 2.0**17)
    ((gr, gi),) = forward([grad], outer, inner, turns)
    advance(ring)
    back_product, back_taps = inverse(
        [(gr * fr + gi * fi, gi * fr - gr * fi), (gr * pr + gi * pi, gi * pr - gr * pi)],
        outer_back, inner_back, turns,
    )
    home_src[1] = pack(back_product, 2.0**8)
    homes[1].start()
    home_src[2] = pack(back_taps, 1.0)
    homes[2].start()
    finish(ring)
    finish(high)

    def columns_of(half):
        total = jnp.zeros((chans, 128), F32)
        for a in range(4):
            left = jnp.concatenate([gbuf[4 * a + j] for j in range(4)], axis=1)
            slots = [lax.rem(4 * half + a + 1 + j, WIDE) for j in range(4)]
            right = jnp.concatenate([tall[slots[j], j] for j in range(4)], axis=0)
            total += dot(left, right)
        return total

    half_src[...] = pack(columns_of(1 - x), 1.0)
    last = wire.go(half_src, half_dst, {"seq": place(1 - x, z, k)})
    mine = columns_of(x)

    def arrived(i, scale):
        homes[i].wait()
        return unpack(home_dst[i].reshape(chans, rows), scale).T

    grad_product = arrived(1, 2.0**8)
    gk_out[...] = (grad_product * v_ref[...].astype(F32)).astype(BF16)
    store(gk_out, gk_hbm)
    gv_out[...] = (grad_product * k_ref[...].astype(F32)).astype(BF16)
    store(gv_out, gv_hbm)
    gf_out[...] = arrived(2, 1.0) * env
    store(gf_out, gf_hbm)
    last.wait_recv()
    gw_out[...] = mine + unpack(half_dst[...], 1.0)
    store(gw_out, gw_hbm)
    for copy in stores:
        copy.wait()
    wire.drain()


def hand_over(*refs):
    src, dst, held, load_sem, store_sem = refs[:5], refs[5:10], refs[10:15], refs[15], refs[16]
    loads = [pltpu.make_async_copy(src[i], held[i], load_sem.at[i]) for i in range(5)]
    stores = [pltpu.make_async_copy(held[i], dst[i], store_sem.at[i]) for i in range(5)]
    for load in loads:
        load.start()
    for load, copy in zip(loads, stores):
        load.wait()
        copy.start()
    for copy in stores:
        copy.wait()


def on_device(query, key, value, filter_raw, rates, out_weight, cotangent):
    rows, chans = query.shape
    fine = chans // PARTS
    tables = transform_tables(rows)
    columns = out_weight.shape[1]
    shape = jax.ShapeDtypeStruct
    block = pltpu.VMEM((rows, chans), BF16)
    piece = (PARTS, fine, rows)
    out_shape = (
        shape((rows, chans), BF16),
        shape((rows, chans), BF16),
        shape((rows, chans), BF16),
        shape((rows, chans), F32),
        shape(out_weight.shape, F32),
    )
    anywhere = pl.BlockSpec(memory_space=pl.ANY)
    results = pl.pallas_call(
        whole,
        out_shape=out_shape,
        in_specs=[anywhere] * 12,
        out_specs=(anywhere,) * 5,
        scratch_shapes=[
            block,
            block,
            block,
            pltpu.VMEM((rows, chans), F32),
            pltpu.VMEM((1, chans), F32),
            *(pltpu.VMEM(t.shape, t.dtype) for t in tables),
            *(pltpu.VMEM(o.shape, o.dtype) for o in out_shape),
            *(pltpu.VMEM((2, *t.shape), BF16) for t in tables[:4]),
            pltpu.VMEM((PARTS, chans, columns), BF16),
            pltpu.VMEM((WIDE, rows, chans), BF16),
            pltpu.VMEM((WIDE, 4, rows, columns), BF16),
            pltpu.VMEM((16, chans, rows), BF16),
            pltpu.VMEM((chans, rows), F32),
            pltpu.VMEM((PARTS, 2 * fine, rows), BF16),
            pltpu.VMEM((PARTS, 2 * fine, rows), BF16),
            pltpu.VMEM(piece, BF16),
            pltpu.VMEM(piece, BF16),
            pltpu.VMEM((3, *piece), BF16),
            pltpu.VMEM((3, *piece), BF16),
            pltpu.VMEM((chans, rows), F32),
            pltpu.VMEM((chans, columns), BF16),
            pltpu.VMEM((chans, columns), BF16),
            pltpu.SemaphoreType.DMA((12,)),
            pltpu.SemaphoreType.DMA((5,)),
            pltpu.SemaphoreType.DMA((94,)),
            pltpu.SemaphoreType.DMA((94,)),
            pltpu.SemaphoreType.DMA((5,)),
            pltpu.SemaphoreType.DMA((5,)),
        ],
        compiler_params=pltpu.CompilerParams(
            collective_id=0, has_side_effects=True, vmem_limit_bytes=63 * 2**20
        ),
        name="whole",
    )(
        query, key, value, filter_raw, rates.reshape(1, chans), out_weight, cotangent,
        *(jnp.asarray(t) for t in tables),
    )
    return pl.pallas_call(
        hand_over,
        out_shape=out_shape,
        in_specs=[anywhere] * 5,
        out_specs=(anywhere,) * 5,
        scratch_shapes=[pltpu.VMEM(o.shape, o.dtype) for o in out_shape]
        + [pltpu.SemaphoreType.DMA((5,)), pltpu.SemaphoreType.DMA((5,))],
        compiler_params=pltpu.CompilerParams(vmem_limit_bytes=63 * 2**20),
        name="hand_over",
    )(*results)


def solution(mesh):
    return jax.shard_map(
        on_device,
        mesh=mesh,
        in_specs=(
            P("seq", "ch"),
            P("seq", "ch"),
            P("seq", "ch"),
            P("seq", "ch"),
            P("ch"),
            P("ch", "seq"),
            P("seq", "ch"),
        ),
        out_specs=(P("seq", "ch"), P("seq", "ch"), P("seq", "ch"), P("seq", "ch"), P("ch", "seq")),
        check_vma=False,
    )
```

```python
import math

import jax
import jax.numpy as jnp
import numpy as np
from jax import lax
from jax.experimental import pallas as pl
from jax.experimental.pallas import tpu as pltpu
from jax.sharding import PartitionSpec as P

MESH = pl.DeviceIdType.MESH
F32 = jnp.float32
BF16 = jnp.bfloat16
NZ, NY, PARTS, WIDE = 8, 4, 32, 8


def transform_tables(rows):
    total = 2 * PARTS * rows
    k1 = np.arange(PARTS + 1)[:, None]
    n1 = np.arange(PARTS)[None, :]
    turn = 2 * math.pi * ((k1 * n1) % (2 * PARTS)) / (2 * PARTS)
    eye = np.eye(8)
    outer = np.kron(np.concatenate([np.cos(turn), -np.sin(turn)[1:-1]], 0), eye)
    weight = np.full((PARTS + 1, 1), 2.0)
    weight[0] = weight[-1] = 1.0
    outer_back = np.concatenate([weight * np.cos(turn), (-weight * np.sin(turn))[1:-1]], 0)
    outer_back = np.kron(outer_back.T / total, eye)
    n2 = np.arange(rows)
    twist = np.repeat(2 * math.pi * (k1 * n2[None, :]) / total, 8, axis=0)
    inner = 2 * math.pi * ((n2[:, None] * n2[None, :]) % rows) / rows
    cos, sin = np.cos(inner), np.sin(inner)
    ahead = np.block([[cos, -sin], [sin, cos]])
    back = np.block([[cos, sin], [-sin, cos]])

    turns = np.stack([np.cos(twist), np.sin(twist)])
    return tuple(np.asarray(m, np.float32) for m in (outer, outer_back, ahead, back, turns))


def halves(x):
    high = x.astype(BF16)
    return high, (x - high.astype(F32)).astype(BF16)


def dot(a, b):
    return jnp.dot(a, b, preferred_element_type=F32)


def dot_const_left(const, x):
    high, low = halves(x)
    return dot(const[0], high) + dot(const[0], low) + dot(const[1], high)


def dot_const_right(x, const):
    high, low = halves(x)
    return dot(high, const[0]) + dot(low, const[0]) + dot(high, const[1])


def forward(signals, outer, inner, turns):
    groups = [x[:, 8 * i : 8 * i + 8, :].reshape(256, 128) for x in signals for i in range(2)]
    y = dot_const_left(outer, jnp.concatenate(groups, axis=1))
    cos, sin = turns[0], turns[1]
    rest = jnp.zeros((8, 128), F32)
    rows = []
    for i in range(len(groups)):
        part = y[:, 128 * i : 128 * i + 128]
        re, im = part[:264], jnp.concatenate([rest, part[264:], rest], axis=0)
        rows.append(jnp.concatenate([re * cos + im * sin, im * cos - re * sin], axis=1))
    z = dot_const_right(jnp.concatenate(rows, axis=0), inner)
    return [(z[528 * i : 528 * i + 528, :128], z[528 * i : 528 * i + 528, 128:]) for i in range(len(signals))]


def inverse(spectra, outer_back, inner_back, turns):
    z = jnp.concatenate([jnp.concatenate(pair, axis=1) for pair in spectra], axis=0)
    z = dot_const_right(z, inner_back)
    cos, sin = turns[0], turns[1]
    columns = []
    for i in range(2 * len(spectra)):
        re, im = z[264 * i : 264 * i + 264, :128], z[264 * i : 264 * i + 264, 128:]
        columns.append(jnp.concatenate([re * cos - im * sin, (im * cos + re * sin)[8:256]], axis=0))
    y = dot_const_left(outer_back, jnp.concatenate(columns, axis=1))
    groups = [y[:, 128 * i : 128 * i + 128].reshape(PARTS, 8, 128) for i in range(len(columns))]
    return [jnp.concatenate(groups[2 * i : 2 * i + 2], axis=1) for i in range(len(spectra))]


def pack(x, scale):
    x = x * scale
    square = x * x
    return (square * (x * jnp.abs(x))).astype(BF16)


def unpack(code, scale):
    code = code.astype(F32)
    size = jnp.sqrt(jnp.sqrt(jnp.abs(code))) * (1.0 / scale)
    return jnp.where(code < 0.0, -size, size)


class Wire:
    def __init__(self, send, recv):
        self.send, self.recv = send, recv
        self.used = 0
        self.groups = []

    def group(self, sent):
        self.groups.append(sent)
        return len(self.groups) - 1

    def slot(self, count=1):
        self.used += count
        return self.used - count

    def go(self, src, dst, to, group, there=None):
        i = self.slot() if there is None else there
        copy = pltpu.make_async_remote_copy(
            src_ref=src,
            dst_ref=dst,
            send_sem=self.send.at[group],
            recv_sem=self.recv.at[i],
            device_id=to,
            device_id_type=MESH,
        )
        copy.start()
        return copy

    def drain(self):
        for i, sent in enumerate(self.groups):
            pltpu.make_async_copy(sent, sent, self.send.at[i]).wait()


def place(x, z, k):
    return x * 16 + lax.rem(z + NZ, NZ) * 2 + k


def gather_seq(wire, buf, x, z, k):
    rows = buf.shape[1]
    cut = rows * 3 // 8
    low, high, full = (0, cut), (cut, rows - cut), (0, rows)

    group = wire.group(buf.at[pl.ds(0, 31)])
    shared = wire.slot()

    def send(src_x, src_z, part, dst, there=None):
        ref = buf.at[place(src_x, src_z, k), pl.ds(*part)]
        return wire.go(ref, ref, {"seq": place(*dst)}, group, there)

    sib, par, right, left = (x, z, 1 - k), (1 - x, z, k), (x, z + 1, k), (x, z - 1, k)
    other = 1 - x
    right_high, left_high = send(x, z, high, right), send(x, z, high, left)
    first = send(x, z, low, par)
    right_low, left_low = send(x, z, low, right), send(x, z, low, left)
    across = [(z, send(x, z, high, par))]
    send(x, z, full, sib, shared)
    yield
    first.wait_recv()
    right_other, left_other = send(other, z, low, right), send(other, z, low, left)
    yield
    for j in (1, 2, 3):
        right_high.wait_recv()
        right_high = send(x, z - j, high, right) if j < 3 else None
        behind = send(x, z - j, high, par)
        left_high.wait_recv()
        left_high = send(x, z + j, high, left)
        ahead = send(x, z + j, high, par)
        right_low.wait_recv()
        right_low = send(x, z - j, low, right)
        send(x, z - j, full, sib, shared)
        left_low.wait_recv()
        left_low = send(x, z + j, low, left) if j < 3 else None
        send(x, z + j, full, sib, shared)
        right_other.wait_recv()
        right_other = send(other, z - j, low if j < 3 else (0, cut // 2), right)
        left_other.wait_recv()
        left_other = send(other, z + j, low if j < 3 else (cut // 2, cut // 2), left)
        for far, copy in across:
            copy.wait_recv()
            send(other, far, full, sib, shared)
        across = [(z - j, behind), (z + j, ahead)]
        yield
    left_high.wait_recv()
    last = send(x, z + 4, high, par)
    send(x, z + 4, high, sib, shared)
    right_low.wait_recv()
    send(x, z + 4, low, sib, shared)
    for far, copy in across:
        copy.wait_recv()
        send(other, far, full, sib, shared)
    right_other.wait_recv()
    left_other.wait_recv()
    send(other, z + 4, low, sib, shared)
    yield
    last.wait_recv()
    send(other, z + 4, high, sib, shared)
    yield
    pltpu.make_async_copy(buf.at[pl.ds(0, 16)], buf.at[pl.ds(0, 16)], wire.recv.at[shared]).wait()
    yield


def ring_z(wire, buf, x, z, k):
    half = buf.shape[1] // 2
    low, high, full = (0, half), (half, half), (0, 2 * half)

    group = wire.group(buf.at[pl.ds(0, 15)])
    shared = wire.slot()

    def ref(far, part):
        return buf.at[lax.rem(z + far + NZ, NZ) * 2 + k, pl.ds(*part)]

    def send(far, part, step):
        r = ref(far, part)
        return wire.go(r, r, {"seq": place(x, z + step, k)}, group)

    def share(far):
        r = ref(far, full)
        wire.go(r, r, {"seq": place(x, z, 1 - k)}, group, shared)

    right, left = send(0, low, 1), send(0, high, -1)
    right2, left2 = send(0, high, 1), send(0, low, -1)
    share(0)
    yield
    for j in (1, 2, 3):
        right.wait_recv()
        right = send(-j, low, 1)
        left.wait_recv()
        left = send(j, high, -1)
        right2.wait_recv()
        right2 = send(-j, high, 1) if j < 3 else None
        left2.wait_recv()
        left2 = send(j, low, -1) if j < 3 else None
        share(-j)
        share(j)
        yield
    right.wait_recv()
    left.wait_recv()
    share(4)
    yield
    pltpu.make_async_copy(buf.at[pl.ds(0, 8)], buf.at[pl.ds(0, 8)], wire.recv.at[shared]).wait()
    yield


def gather_ch(wire, buf, y, x):
    half = buf.shape[1] // 2

    group = wire.group(buf.at[pl.ds(0, 7)])

    def send(src_y, src_x, part, dst_y, dst_x):
        ref = buf.at[lax.rem(src_y + NY, NY) * 2 + src_x, pl.ds(*part)]
        return wire.go(ref, ref, {"ch": lax.rem(dst_y + NY, NY) * 2 + dst_x}, group)

    full, low, high = (0, 2 * half), (0, half), (half, half)
    first = send(y, x, full, y, 1 - x)
    near = [send(y, x, full, y + 1, x), send(y, x, full, y - 1, x)]
    yield
    first.wait_recv()
    near += [send(y, 1 - x, full, y + 1, x), send(y, 1 - x, full, y - 1, x)]
    yield
    far = []
    for i, copy in enumerate(near):
        copy.wait_recv()
        whose = x if i < 2 else 1 - x
        if i % 2 == 0:
            far.append(send(y - 1, whose, low, y + 1, x))
        else:
            far.append(send(y + 1, whose, high, y - 1, x))
    yield
    for copy in far:
        copy.wait_recv()
    yield


def advance(steps, count=1):
    for _ in range(count):
        next(steps, None)


def finish(steps):
    for _ in steps:
        pass


class Swap:
    def __init__(self, src, dst, send, recv, me):
        self.src, self.dst, self.send, self.recv, self.me = src, dst, send, recv, me

    def copy(self, d):
        target = lax.rem(self.me + d, PARTS)
        return pltpu.make_async_remote_copy(
            src_ref=self.src.at[target],
            dst_ref=self.dst.at[self.me],
            send_sem=self.send,
            recv_sem=self.recv,
            device_id={"seq": target},
            device_id_type=MESH,
        )

    def start(self, low=1, high=PARTS):
        @pl.loop(low, high)
        def _(d):
            self.copy(d).start()

        if low == 1:
            self.dst[self.me] = self.src[self.me]

    def wait(self):
        for ref, sem in ((self.dst, self.recv), (self.src, self.send)):
            all_pieces = ref.at[pl.ds(0, PARTS - 1)]
            pltpu.make_async_copy(all_pieces, all_pieces, sem).wait()


def envelope_of(rates, me, rows):
    total = rows * PARTS
    spot = me * rows + lax.broadcasted_iota(jnp.int32, (rows, 1), 0)
    spot = spot.astype(F32) / total
    scaling = jnp.sqrt(2.0 * rates / (total * (1.0 - jnp.exp(-2.0 * rates))))
    return jnp.exp(-spot * rates) * scaling


def whole(
    q_hbm, k_hbm, v_hbm, f_hbm, r_hbm, w_hbm, c_hbm,
    outer_hbm, outer_back_hbm, inner_hbm, inner_back_hbm, turns_hbm,
    gq_hbm, gk_hbm, gv_hbm, gf_hbm, gw_hbm,
    q_ref, k_ref, v_ref, f_ref, r_ref, outer_ref, outer_back_ref, inner_ref, inner_back_ref, turns,
    gq_out, gk_out, gv_out, gf_out, gw_out, outer, outer_back, inner, inner_back,
    wbuf, cbuf, tall, gbuf, rate_ref,
    in_src, in_dst, gm_src, gm_dst, home_src, home_dst, qt_ref, half_src, half_dst,
    load_sem, store_sem, wire_send, wire_recv, swap_send, swap_recv,
):
    me, ch = lax.axis_index("seq"), lax.axis_index("ch")
    x, z, k = me // 16, lax.rem(me // 2, NZ), lax.rem(me, 2)
    zk = lax.rem(me, 16)
    y, xl = ch // 2, lax.rem(ch, 2)
    rows, chans = q_ref.shape
    fine = chans // PARTS
    wire = Wire(wire_send, wire_recv)

    loads = [
        pltpu.make_async_copy(src, dst, load_sem.at[i])
        for i, (src, dst) in enumerate(
            (
                (w_hbm, wbuf.at[me]),
                (c_hbm, cbuf.at[ch]),
                (k_hbm, k_ref),
                (v_hbm, v_ref),
                (f_hbm, f_ref),
                (q_hbm, q_ref),
                (r_hbm, r_ref),
                (outer_hbm, outer_ref),
                (outer_back_hbm, outer_back_ref),
                (inner_hbm, inner_ref),
                (inner_back_hbm, inner_back_ref),
                (turns_hbm, turns),
            )
        )
    ]
    for load in loads:
        load.start()

    spot = (ch // 4) * 16 + zk
    keeper = lax.rem(spot // 4 + 1 + lax.rem(spot, 4), WIDE)
    targets = [{"seq": x * 16 + lax.rem(ch, 4) * 4 + i, "ch": keeper} for i in range(4)]
    sources = []
    for j in range(4):
        theirs = 4 * lax.rem(ch - 1 - j + WIDE, WIDE) + j
        sources.append(
            {"seq": x * 16 + lax.rem(theirs, 16), "ch": (theirs // 16) * 4 + zk // 4}
        )
    around = [
        {"ch": y * 2 + 1 - xl},
        {"ch": lax.rem(y + 1, NY) * 2 + xl},
        {"ch": lax.rem(y + NY - 1, NY) * 2 + xl},
    ]
    greeted = targets + sources + around
    barrier = pltpu.get_barrier_semaphore()

    @pl.loop(1, PARTS)
    def _(d):
        pl.semaphore_signal(
            barrier, inc=1, device_id={"seq": lax.rem(me + d, PARTS)}, device_id_type=MESH
        )

    for to in greeted:
        pl.semaphore_signal(barrier, inc=1, device_id=to, device_id_type=MESH)


    def turned(value):
        return value.T.reshape(PARTS, fine, rows)

    def swap(i, src, dst):
        return Swap(src, dst, swap_send.at[i], swap_recv.at[i], me)

    stores = []

    def store(src, dst):
        copy = pltpu.make_async_copy(src, dst, store_sem.at[len(stores)])
        copy.start()
        stores.append(copy)

    early = swap(0, in_src, in_dst)
    late = swap(1, gm_src, gm_dst)
    homes = [swap(2 + i, home_src.at[i], home_dst.at[i]) for i in range(3)]

    loads[0].wait()
    loads[1].wait()
    pl.semaphore_wait(barrier, PARTS - 1 + len(greeted))
    weights = gather_seq(wire, wbuf, x, z, k)
    advance(weights)
    wide = gather_ch(wire, cbuf, y, xl)
    advance(wide)
    for load in loads[2:5]:
        load.wait()
    in_src[:, 0:16] = pack(turned(k_ref[...].astype(F32) * v_ref[...].astype(F32)), 2.0**25)
    in_src[:, 16:32] = pack(turned(f_ref[...]), 2.0**28)
    early.start()
    advance(weights)
    advance(wide)
    for load in loads[5:]:
        load.wait()
    qt_ref[...] = q_ref[...].astype(F32).T
    for wide_const, const in (
        (outer_ref, outer), (outer_back_ref, outer_back), (inner_ref, inner), (inner_back_ref, inner_back)
    ):
        const[0], const[1] = halves(wide_const[...])
    rate_ref[...] = jnp.broadcast_to(r_ref[...], (rows, chans)).T
    env = envelope_of(r_ref[...], me, rows)
    own_rates = rate_ref[pl.ds(me * fine, fine), :]
    lanes = lax.broadcasted_iota(jnp.int32, (fine, rows), 1)
    span = float(rows * PARTS)
    own_scaling = jnp.sqrt(2.0 * own_rates / (span * (1.0 - jnp.exp(-2.0 * own_rates))))
    envelope = jnp.stack(
        [
            jnp.exp(-((lanes + block * rows).astype(F32) / span) * own_rates) * own_scaling
            for block in range(PARTS)
        ]
    )
    advance(weights)
    advance(weights)
    early.wait()
    product = unpack(in_dst[:, 0:16], 2.0**25)
    filt = unpack(in_dst[:, 16:32], 2.0**28) * envelope
    (pr, pi), (fr, fi) = forward([product, filt], outer, inner, turns)
    advance(weights)
    advance(wide)
    (mixed,) = inverse([(pr * fr - pi * fi, pr * fi + pi * fr)], outer_back, inner_back, turns)
    home_src[0] = pack(mixed, 2.0**17)
    homes[0].start()
    base = wire.slot(4)
    columns_sent = wire.group(tall.at[0])
    for i, to in enumerate(targets):
        src = cbuf.at[ch, :, pl.ds(i * 128, 128)]
        wire.go(src, tall.at[keeper, lax.rem(me, 4)], to, columns_sent, base + lax.rem(me, 4))
    advance(weights)
    finish(wide)
    advance(weights)
    homes[0].wait()
    mixed_home = unpack(home_dst[0].reshape(chans, rows), 2.0**17)
    gbuf[zk] = (qt_ref[...] * mixed_home).astype(BF16)
    ring = ring_z(wire, gbuf, x, z, k)
    advance(ring)
    finish(weights)
    for j in range(4):
        pltpu.make_async_copy(tall.at[0, 0], tall.at[0, 0], wire_recv.at[base + j]).wait()
    high = gather_ch(wire, tall, y, xl)
    advance(high)
    total = jnp.zeros((rows, chans), F32)
    for h in range(WIDE):
        part = jnp.concatenate([wbuf[4 * h + i] for i in range(4)], axis=1)
        total += lax.dot_general(
            cbuf[h], part, (((1,), (1,)), ((), ())), preferred_element_type=F32
        )
    gm_src[...] = pack(turned(q_ref[...].astype(F32) * total), 2.0**17)
    late.start()
    advance(ring)
    advance(high)
    gq_out[...] = (mixed_home.T * total).astype(BF16)
    store(gq_out, gq_hbm)
    advance(ring)
    advance(high)
    late.wait()
    grad = unpack(gm_dst[...], 2.0**17)
    ((gr, gi),) = forward([grad], outer, inner, turns)
    advance(ring)
    back_product, back_taps = inverse(
        [(gr * fr + gi * fi, gi * fr - gr * fi), (gr * pr + gi * pi, gi * pr - gr * pi)],
        outer_back, inner_back, turns,
    )
    home_src[1] = pack(back_product, 2.0**8)
    homes[1].start()
    home_src[2] = pack(back_taps, 1.0)
    homes[2].start()
    finish(ring)
    finish(high)

    def columns_of(half):
        total = jnp.zeros((chans, 128), F32)
        for a in range(4):
            left = jnp.concatenate([gbuf[4 * a + j] for j in range(4)], axis=1)
            slots = [lax.rem(4 * half + a + 1 + j, WIDE) for j in range(4)]
            right = jnp.concatenate([tall[slots[j], j] for j in range(4)], axis=0)
            total += dot(left, right)
        return total

    half_src[...] = pack(columns_of(1 - x), 1.0)
    last = wire.go(
        half_src, half_dst, {"seq": place(1 - x, z, k)}, wire.group(half_src)
    )
    mine = columns_of(x)

    def arrived(i, scale):
        homes[i].wait()
        return unpack(home_dst[i].reshape(chans, rows), scale).T

    grad_product = arrived(1, 2.0**8)
    gk_out[...] = (grad_product * v_ref[...].astype(F32)).astype(BF16)
    store(gk_out, gk_hbm)
    gv_out[...] = (grad_product * k_ref[...].astype(F32)).astype(BF16)
    store(gv_out, gv_hbm)
    gf_out[...] = arrived(2, 1.0) * env
    store(gf_out, gf_hbm)
    last.wait_recv()
    gw_out[...] = mine + unpack(half_dst[...], 1.0)
    store(gw_out, gw_hbm)
    for copy in stores:
        copy.wait()
    wire.drain()


def hand_over(*refs):
    src, dst, held, load_sem, store_sem = refs[:5], refs[5:10], refs[10:15], refs[15], refs[16]
    loads = [pltpu.make_async_copy(src[i], held[i], load_sem.at[i]) for i in range(5)]
    stores = [pltpu.make_async_copy(held[i], dst[i], store_sem.at[i]) for i in range(5)]
    for load in loads:
        load.start()
    for load, copy in zip(loads, stores):
        load.wait()
        copy.start()
    for copy in stores:
        copy.wait()


def on_device(query, key, value, filter_raw, rates, out_weight, cotangent):
    rows, chans = query.shape
    fine = chans // PARTS
    tables = transform_tables(rows)
    columns = out_weight.shape[1]
    shape = jax.ShapeDtypeStruct
    block = pltpu.VMEM((rows, chans), BF16)
    piece = (PARTS, fine, rows)
    out_shape = (
        shape((rows, chans), BF16),
        shape((rows, chans), BF16),
        shape((rows, chans), BF16),
        shape((rows, chans), F32),
        shape(out_weight.shape, F32),
    )
    anywhere = pl.BlockSpec(memory_space=pl.ANY)
    results = pl.pallas_call(
        whole,
        out_shape=out_shape,
        in_specs=[anywhere] * 12,
        out_specs=(anywhere,) * 5,
        scratch_shapes=[
            block,
            block,
            block,
            pltpu.VMEM((rows, chans), F32),
            pltpu.VMEM((1, chans), F32),
            *(pltpu.VMEM(t.shape, t.dtype) for t in tables),
            *(pltpu.VMEM(o.shape, o.dtype) for o in out_shape),
            *(pltpu.VMEM((2, *t.shape), BF16) for t in tables[:4]),
            pltpu.VMEM((PARTS, chans, columns), BF16),
            pltpu.VMEM((WIDE, rows, chans), BF16),
            pltpu.VMEM((WIDE, 4, rows, columns), BF16),
            pltpu.VMEM((16, chans, rows), BF16),
            pltpu.VMEM((chans, rows), F32),
            pltpu.VMEM((PARTS, 2 * fine, rows), BF16),
            pltpu.VMEM((PARTS, 2 * fine, rows), BF16),
            pltpu.VMEM(piece, BF16),
            pltpu.VMEM(piece, BF16),
            pltpu.VMEM((3, *piece), BF16),
            pltpu.VMEM((3, *piece), BF16),
            pltpu.VMEM((chans, rows), F32),
            pltpu.VMEM((chans, columns), BF16),
            pltpu.VMEM((chans, columns), BF16),
            pltpu.SemaphoreType.DMA((12,)),
            pltpu.SemaphoreType.DMA((5,)),
            pltpu.SemaphoreType.DMA((6,)),
            pltpu.SemaphoreType.DMA((70,)),
            pltpu.SemaphoreType.DMA((5,)),
            pltpu.SemaphoreType.DMA((5,)),
        ],
        compiler_params=pltpu.CompilerParams(
            collective_id=0, has_side_effects=True, vmem_limit_bytes=63 * 2**20
        ),
        name="whole",
    )(
        query, key, value, filter_raw, rates.reshape(1, chans), out_weight, cotangent,
        *(jnp.asarray(t) for t in tables),
    )
    return pl.pallas_call(
        hand_over,
        out_shape=out_shape,
        in_specs=[anywhere] * 5,
        out_specs=(anywhere,) * 5,
        scratch_shapes=[pltpu.VMEM(o.shape, o.dtype) for o in out_shape]
        + [pltpu.SemaphoreType.DMA((5,)), pltpu.SemaphoreType.DMA((5,))],
        compiler_params=pltpu.CompilerParams(vmem_limit_bytes=63 * 2**20),
        name="hand_over",
    )(*results)


def solution(mesh):
    return jax.shard_map(
        on_device,
        mesh=mesh,
        in_specs=(
            P("seq", "ch"),
            P("seq", "ch"),
            P("seq", "ch"),
            P("seq", "ch"),
            P("ch"),
            P("ch", "seq"),
            P("seq", "ch"),
        ),
        out_specs=(P("seq", "ch"), P("seq", "ch"), P("seq", "ch"), P("seq", "ch"), P("ch", "seq")),
        check_vma=False,
    )
```

```python
import math

import jax
import jax.numpy as jnp
import numpy as np
from jax import lax
from jax.experimental import pallas as pl
from jax.experimental.pallas import tpu as pltpu
from jax.sharding import PartitionSpec as P

MESH = pl.DeviceIdType.MESH
F32 = jnp.float32
BF16 = jnp.bfloat16
NZ, NY, PARTS, WIDE = 8, 4, 32, 8


def transform_tables(rows):
    total = 2 * PARTS * rows
    k1 = np.arange(PARTS + 1)[:, None]
    n1 = np.arange(PARTS)[None, :]
    turn = 2 * math.pi * ((k1 * n1) % (2 * PARTS)) / (2 * PARTS)
    eye = np.eye(8)
    outer = np.kron(np.concatenate([np.cos(turn), -np.sin(turn)[1:-1]], 0), eye)
    weight = np.full((PARTS + 1, 1), 2.0)
    weight[0] = weight[-1] = 1.0
    outer_back = np.concatenate([weight * np.cos(turn), (-weight * np.sin(turn))[1:-1]], 0)
    outer_back = np.kron(outer_back.T / total, eye)
    n2 = np.arange(rows)
    twist = np.repeat(2 * math.pi * (k1 * n2[None, :]) / total, 8, axis=0)
    inner = 2 * math.pi * ((n2[:, None] * n2[None, :]) % rows) / rows
    cos, sin = np.cos(inner), np.sin(inner)
    ahead = np.block([[cos, -sin], [sin, cos]])
    back = np.block([[cos, sin], [-sin, cos]])

    turns = np.stack([np.cos(twist), np.sin(twist)])
    return tuple(np.asarray(m, np.float32) for m in (outer, outer_back, ahead, back, turns))


def halves(x):
    high = x.astype(BF16)
    return high, (x - high.astype(F32)).astype(BF16)


def dot(a, b):
    return jnp.dot(a, b, preferred_element_type=F32)


def dot_const_left(const, x):
    high, low = halves(x)
    return dot(const[0], high) + dot(const[0], low) + dot(const[1], high)


def dot_const_right(x, const):
    high, low = halves(x)
    return dot(high, const[0]) + dot(low, const[0]) + dot(high, const[1])


def forward(signals, outer, inner, turns):
    groups = [x[:, 8 * i : 8 * i + 8, :].reshape(256, 128) for x in signals for i in range(2)]
    y = dot_const_left(outer, jnp.concatenate(groups, axis=1))
    cos, sin = turns[0], turns[1]
    rest = jnp.zeros((8, 128), F32)
    rows = []
    for i in range(len(groups)):
        part = y[:, 128 * i : 128 * i + 128]
        re, im = part[:264], jnp.concatenate([rest, part[264:], rest], axis=0)
        rows.append(jnp.concatenate([re * cos + im * sin, im * cos - re * sin], axis=1))
    z = dot_const_right(jnp.concatenate(rows, axis=0), inner)
    return [(z[528 * i : 528 * i + 528, :128], z[528 * i : 528 * i + 528, 128:]) for i in range(len(signals))]


def inverse(spectra, outer_back, inner_back, turns):
    z = jnp.concatenate([jnp.concatenate(pair, axis=1) for pair in spectra], axis=0)
    z = dot_const_right(z, inner_back)
    cos, sin = turns[0], turns[1]
    columns = []
    for i in range(2 * len(spectra)):
        re, im = z[264 * i : 264 * i + 264, :128], z[264 * i : 264 * i + 264, 128:]
        columns.append(jnp.concatenate([re * cos - im * sin, (im * cos + re * sin)[8:256]], axis=0))
    y = dot_const_left(outer_back, jnp.concatenate(columns, axis=1))
    groups = [y[:, 128 * i : 128 * i + 128].reshape(PARTS, 8, 128) for i in range(len(columns))]
    return [jnp.concatenate(groups[2 * i : 2 * i + 2], axis=1) for i in range(len(spectra))]


def pack(x, scale):
    x = x * scale
    square = x * x
    return (square * (x * jnp.abs(x))).astype(BF16)


def unpack(code, scale):
    code = code.astype(F32)
    size = jnp.sqrt(jnp.sqrt(jnp.abs(code))) * (1.0 / scale)
    return jnp.where(code < 0.0, -size, size)


class Wire:
    def __init__(self, send, recv):
        self.send, self.recv = send, recv
        self.used = 0
        self.groups = []

    def group(self, sent):
        self.groups.append(sent)
        return len(self.groups) - 1

    def slot(self, count=1):
        self.used += count
        return self.used - count

    def go(self, src, dst, to, group, there=None):
        i = self.slot() if there is None else there
        copy = pltpu.make_async_remote_copy(
            src_ref=src,
            dst_ref=dst,
            send_sem=self.send.at[group],
            recv_sem=self.recv.at[i],
            device_id=to,
            device_id_type=MESH,
        )
        copy.start()
        return copy

    def drain(self):
        for i, sent in enumerate(self.groups):
            pltpu.make_async_copy(sent, sent, self.send.at[i]).wait()


def place(x, z, k):
    return x * 16 + lax.rem(z + NZ, NZ) * 2 + k


def gather_seq(wire, buf, x, z, k):
    rows = buf.shape[1]
    cut = rows * 3 // 8
    low, high, full = (0, cut), (cut, rows - cut), (0, rows)

    group = wire.group(buf.at[pl.ds(0, 31)])
    shared = wire.slot()

    def send(src_x, src_z, part, dst, there=None):
        ref = buf.at[place(src_x, src_z, k), pl.ds(*part)]
        return wire.go(ref, ref, {"seq": place(*dst)}, group, there)

    sib, par, right, left = (x, z, 1 - k), (1 - x, z, k), (x, z + 1, k), (x, z - 1, k)
    other = 1 - x
    right_high, left_high = send(x, z, high, right), send(x, z, high, left)
    first = send(x, z, low, par)
    right_low, left_low = send(x, z, low, right), send(x, z, low, left)
    across = [(z, send(x, z, high, par))]
    send(x, z, full, sib, shared)
    yield
    first.wait_recv()
    right_other, left_other = send(other, z, low, right), send(other, z, low, left)
    yield
    for j in (1, 2, 3):
        right_high.wait_recv()
        right_high = send(x, z - j, high, right) if j < 3 else None
        behind = send(x, z - j, high, par)
        left_high.wait_recv()
        left_high = send(x, z + j, high, left)
        ahead = send(x, z + j, high, par)
        right_low.wait_recv()
        right_low = send(x, z - j, low, right)
        send(x, z - j, full, sib, shared)
        left_low.wait_recv()
        left_low = send(x, z + j, low, left) if j < 3 else None
        send(x, z + j, full, sib, shared)
        right_other.wait_recv()
        right_other = send(other, z - j, low if j < 3 else (0, cut // 2), right)
        left_other.wait_recv()
        left_other = send(other, z + j, low if j < 3 else (cut // 2, cut // 2), left)
        for far, copy in across:
            copy.wait_recv()
            send(other, far, full, sib, shared)
        across = [(z - j, behind), (z + j, ahead)]
        yield
    left_high.wait_recv()
    last = send(x, z + 4, high, par)
    send(x, z + 4, high, sib, shared)
    right_low.wait_recv()
    send(x, z + 4, low, sib, shared)
    for far, copy in across:
        copy.wait_recv()
        send(other, far, full, sib, shared)
    right_other.wait_recv()
    left_other.wait_recv()
    send(other, z + 4, low, sib, shared)
    yield
    last.wait_recv()
    send(other, z + 4, high, sib, shared)
    yield
    pltpu.make_async_copy(buf.at[pl.ds(0, 16)], buf.at[pl.ds(0, 16)], wire.recv.at[shared]).wait()
    yield


def ring_z(wire, buf, x, z, k):
    half = buf.shape[1] // 2
    low, high, full = (0, half), (half, half), (0, 2 * half)

    group = wire.group(buf.at[pl.ds(0, 15)])
    shared = wire.slot()

    def ref(far, part):
        return buf.at[lax.rem(z + far + NZ, NZ) * 2 + k, pl.ds(*part)]

    def send(far, part, step):
        r = ref(far, part)
        return wire.go(r, r, {"seq": place(x, z + step, k)}, group)

    def share(far):
        r = ref(far, full)
        wire.go(r, r, {"seq": place(x, z, 1 - k)}, group, shared)

    right, left = send(0, low, 1), send(0, high, -1)
    right2, left2 = send(0, high, 1), send(0, low, -1)
    share(0)
    yield
    for j in (1, 2, 3):
        right.wait_recv()
        right = send(-j, low, 1)
        left.wait_recv()
        left = send(j, high, -1)
        right2.wait_recv()
        right2 = send(-j, high, 1) if j < 3 else None
        left2.wait_recv()
        left2 = send(j, low, -1) if j < 3 else None
        share(-j)
        share(j)
        yield
    right.wait_recv()
    left.wait_recv()
    share(4)
    yield
    pltpu.make_async_copy(buf.at[pl.ds(0, 8)], buf.at[pl.ds(0, 8)], wire.recv.at[shared]).wait()
    yield


def gather_ch(wire, buf, y, x):
    half = buf.shape[1] // 2

    group = wire.group(buf.at[pl.ds(0, 7)])

    def send(src_y, src_x, part, dst_y, dst_x):
        ref = buf.at[lax.rem(src_y + NY, NY) * 2 + src_x, pl.ds(*part)]
        return wire.go(ref, ref, {"ch": lax.rem(dst_y + NY, NY) * 2 + dst_x}, group)

    full, low, high = (0, 2 * half), (0, half), (half, half)
    first = send(y, x, full, y, 1 - x)
    near = [send(y, x, full, y + 1, x), send(y, x, full, y - 1, x)]
    yield
    first.wait_recv()
    near += [send(y, 1 - x, full, y + 1, x), send(y, 1 - x, full, y - 1, x)]
    yield
    far = []
    for i, copy in enumerate(near):
        copy.wait_recv()
        whose = x if i < 2 else 1 - x
        if i % 2 == 0:
            far.append(send(y - 1, whose, low, y + 1, x))
        else:
            far.append(send(y + 1, whose, high, y - 1, x))
    yield
    for copy in far:
        copy.wait_recv()
    yield


def advance(steps, count=1):
    for _ in range(count):
        next(steps, None)


def finish(steps):
    for _ in steps:
        pass


class Swap:
    def __init__(self, src, dst, send, recv, me):
        self.src, self.dst, self.send, self.recv, self.me = src, dst, send, recv, me

    def copy(self, d):
        target = lax.rem(self.me + d, PARTS)
        return pltpu.make_async_remote_copy(
            src_ref=self.src.at[target],
            dst_ref=self.dst.at[self.me],
            send_sem=self.send,
            recv_sem=self.recv,
            device_id={"seq": target},
            device_id_type=MESH,
        )

    def start(self, low=1, high=PARTS):
        @pl.loop(low, high)
        def _(d):
            self.copy(d).start()

        if low == 1:
            self.dst[self.me] = self.src[self.me]

    def wait(self):
        for ref, sem in ((self.dst, self.recv), (self.src, self.send)):
            all_pieces = ref.at[pl.ds(0, PARTS - 1)]
            pltpu.make_async_copy(all_pieces, all_pieces, sem).wait()


def envelope_of(rates, me, rows):
    total = rows * PARTS
    spot = me * rows + lax.broadcasted_iota(jnp.int32, (rows, 1), 0)
    spot = spot.astype(F32) / total
    scaling = jnp.sqrt(2.0 * rates / (total * (1.0 - jnp.exp(-2.0 * rates))))
    return jnp.exp(-spot * rates) * scaling


def whole(
    q_hbm, k_hbm, v_hbm, f_hbm, r_hbm, w_hbm, c_hbm,
    outer_hbm, outer_back_hbm, inner_hbm, inner_back_hbm, turns_hbm,
    gq_hbm, gk_hbm, gv_hbm, gf_hbm, gw_hbm,
    q_ref, k_ref, v_ref, f_ref, r_ref, outer_ref, outer_back_ref, inner_ref, inner_back_ref, turns,
    gq_out, gk_out, gv_out, gf_out, gw_out, outer, outer_back, inner, inner_back,
    wbuf, cbuf, tall, gbuf, rate_ref,
    in_src, in_dst, gm_src, gm_dst, home_src, home_dst, pair_src, pair_dst, qt_ref, half_src, half_dst,
    load_sem, store_sem, wire_send, wire_recv, swap_send, swap_recv,
):
    me, ch = lax.axis_index("seq"), lax.axis_index("ch")
    x, z, k = me // 16, lax.rem(me // 2, NZ), lax.rem(me, 2)
    zk = lax.rem(me, 16)
    y, xl = ch // 2, lax.rem(ch, 2)
    rows, chans = q_ref.shape
    fine = chans // PARTS
    wire = Wire(wire_send, wire_recv)

    loads = [
        pltpu.make_async_copy(src, dst, load_sem.at[i])
        for i, (src, dst) in enumerate(
            (
                (w_hbm, wbuf.at[me]),
                (c_hbm, cbuf.at[ch]),
                (k_hbm, k_ref),
                (v_hbm, v_ref),
                (f_hbm, f_ref),
                (q_hbm, q_ref),
                (r_hbm, r_ref),
                (outer_hbm, outer_ref),
                (outer_back_hbm, outer_back_ref),
                (inner_hbm, inner_ref),
                (inner_back_hbm, inner_back_ref),
                (turns_hbm, turns),
            )
        )
    ]
    for load in loads:
        load.start()

    spot = (ch // 4) * 16 + zk
    keeper = lax.rem(spot // 4 + 1 + lax.rem(spot, 4), WIDE)
    targets = [{"seq": x * 16 + lax.rem(ch, 4) * 4 + i, "ch": keeper} for i in range(4)]
    sources = []
    for j in range(4):
        theirs = 4 * lax.rem(ch - 1 - j + WIDE, WIDE) + j
        sources.append(
            {"seq": x * 16 + lax.rem(theirs, 16), "ch": (theirs // 16) * 4 + zk // 4}
        )
    around = [
        {"ch": y * 2 + 1 - xl},
        {"ch": lax.rem(y + 1, NY) * 2 + xl},
        {"ch": lax.rem(y + NY - 1, NY) * 2 + xl},
    ]
    greeted = targets + sources + around
    barrier = pltpu.get_barrier_semaphore()

    @pl.loop(1, PARTS)
    def _(d):
        pl.semaphore_signal(
            barrier, inc=1, device_id={"seq": lax.rem(me + d, PARTS)}, device_id_type=MESH
        )

    for to in greeted:
        pl.semaphore_signal(barrier, inc=1, device_id=to, device_id_type=MESH)


    def turned(value):
        return value.T.reshape(PARTS, fine, rows)

    def swap(i, src, dst):
        return Swap(src, dst, swap_send.at[i], swap_recv.at[i], me)

    stores = []

    def store(src, dst):
        copy = pltpu.make_async_copy(src, dst, store_sem.at[len(stores)])
        copy.start()
        stores.append(copy)

    early = swap(0, in_src, in_dst)
    late = swap(1, gm_src, gm_dst)
    home = swap(2, home_src, home_dst)
    pair = swap(3, pair_src, pair_dst)

    loads[0].wait()
    loads[1].wait()
    pl.semaphore_wait(barrier, PARTS - 1 + len(greeted))
    weights = gather_seq(wire, wbuf, x, z, k)
    advance(weights)
    wide = gather_ch(wire, cbuf, y, xl)
    advance(wide)
    for load in loads[2:5]:
        load.wait()
    in_src[:, 0:16] = pack(turned(k_ref[...].astype(F32) * v_ref[...].astype(F32)), 2.0**25)
    in_src[:, 16:32] = pack(turned(f_ref[...]), 2.0**28)
    early.start()
    advance(weights)
    advance(wide)
    for load in loads[5:]:
        load.wait()
    qt_ref[...] = q_ref[...].astype(F32).T
    for wide_const, const in (
        (outer_ref, outer), (outer_back_ref, outer_back), (inner_ref, inner), (inner_back_ref, inner_back)
    ):
        const[0], const[1] = halves(wide_const[...])
    rate_ref[...] = jnp.broadcast_to(r_ref[...], (rows, chans)).T
    env = envelope_of(r_ref[...], me, rows)
    own_rates = rate_ref[pl.ds(me * fine, fine), :]
    lanes = lax.broadcasted_iota(jnp.int32, (fine, rows), 1)
    span = float(rows * PARTS)
    own_scaling = jnp.sqrt(2.0 * own_rates / (span * (1.0 - jnp.exp(-2.0 * own_rates))))
    envelope = jnp.stack(
        [
            jnp.exp(-((lanes + block * rows).astype(F32) / span) * own_rates) * own_scaling
            for block in range(PARTS)
        ]
    )
    advance(weights)
    advance(weights)
    early.wait()
    product = unpack(in_dst[:, 0:16], 2.0**25)
    filt = unpack(in_dst[:, 16:32], 2.0**28) * envelope
    (pr, pi), (fr, fi) = forward([product, filt], outer, inner, turns)
    advance(weights)
    advance(wide)
    (mixed,) = inverse([(pr * fr - pi * fi, pr * fi + pi * fr)], outer_back, inner_back, turns)
    home_src[...] = pack(mixed, 2.0**17)
    home.start()
    base = wire.slot(4)
    columns_sent = wire.group(tall.at[0])
    for i, to in enumerate(targets):
        src = cbuf.at[ch, :, pl.ds(i * 128, 128)]
        wire.go(src, tall.at[keeper, lax.rem(me, 4)], to, columns_sent, base + lax.rem(me, 4))
    advance(weights)
    finish(wide)
    advance(weights)
    home.wait()
    mixed_home = unpack(home_dst[...].reshape(chans, rows), 2.0**17)
    gbuf[zk] = (qt_ref[...] * mixed_home).astype(BF16)
    ring = ring_z(wire, gbuf, x, z, k)
    advance(ring)
    finish(weights)
    for j in range(4):
        pltpu.make_async_copy(tall.at[0, 0], tall.at[0, 0], wire_recv.at[base + j]).wait()
    high = gather_ch(wire, tall, y, xl)
    advance(high)
    total = jnp.zeros((rows, chans), F32)
    for h in range(WIDE):
        part = jnp.concatenate([wbuf[4 * h + i] for i in range(4)], axis=1)
        total += lax.dot_general(
            cbuf[h], part, (((1,), (1,)), ((), ())), preferred_element_type=F32
        )
    gm_src[...] = pack(turned(q_ref[...].astype(F32) * total), 2.0**17)
    late.start()
    advance(ring)
    advance(high)
    advance(ring)
    advance(high)
    gq_out[...] = (mixed_home.T * total).astype(BF16)
    store(gq_out, gq_hbm)
    late.wait()
    grad = unpack(gm_dst[...], 2.0**17)
    ((gr, gi),) = forward([grad], outer, inner, turns)
    advance(ring)
    back_product, back_taps = inverse(
        [(gr * fr + gi * fi, gi * fr - gr * fi), (gr * pr + gi * pi, gi * pr - gr * pi)],
        outer_back, inner_back, turns,
    )
    pair_src[:, 0:16] = pack(back_product, 2.0**8)
    pair_src[:, 16:32] = pack(back_taps, 1.0)
    pair.start()
    finish(ring)
    finish(high)

    def columns_of(half, low, count):
        total = jnp.zeros((count, 128), F32)
        for a in range(4):
            left = jnp.concatenate([gbuf[4 * a + j, low : low + count] for j in range(4)], axis=1)
            slots = [lax.rem(4 * half + a + 1 + j, WIDE) for j in range(4)]
            right = jnp.concatenate([tall[slots[j], j] for j in range(4)], axis=0)
            total += dot(left, right)
        return total

    half_sent = wire.group(half_src)
    last = []
    for low in (0, chans // 2):
        part = pl.ds(low, chans // 2)
        half_src[part] = pack(columns_of(1 - x, low, chans // 2), 1.0)
        last.append(
            wire.go(half_src.at[part], half_dst.at[part], {"seq": place(1 - x, z, k)}, half_sent)
        )
    mine = columns_of(x, 0, chans)

    def arrived(i, scale):
        return unpack(pair_dst[:, 16 * i : 16 * i + 16].reshape(chans, rows), scale).T

    pair.wait()
    grad_product = arrived(0, 2.0**8)
    gk_out[...] = (grad_product * v_ref[...].astype(F32)).astype(BF16)
    store(gk_out, gk_hbm)
    gv_out[...] = (grad_product * k_ref[...].astype(F32)).astype(BF16)
    store(gv_out, gv_hbm)
    gf_out[...] = arrived(1, 1.0) * env
    store(gf_out, gf_hbm)
    for copy in last:
        copy.wait_recv()
    gw_out[...] = mine + unpack(half_dst[...], 1.0)
    store(gw_out, gw_hbm)
    for copy in stores:
        copy.wait()
    wire.drain()


def hand_over(*refs):
    src, dst, held, load_sem, store_sem = refs[:5], refs[5:10], refs[10:15], refs[15], refs[16]
    loads = [pltpu.make_async_copy(src[i], held[i], load_sem.at[i]) for i in range(5)]
    stores = [pltpu.make_async_copy(held[i], dst[i], store_sem.at[i]) for i in range(5)]
    for load in loads:
        load.start()
    for load, copy in zip(loads, stores):
        load.wait()
        copy.start()
    for copy in stores:
        copy.wait()


def on_device(query, key, value, filter_raw, rates, out_weight, cotangent):
    rows, chans = query.shape
    fine = chans // PARTS
    tables = transform_tables(rows)
    columns = out_weight.shape[1]
    shape = jax.ShapeDtypeStruct
    block = pltpu.VMEM((rows, chans), BF16)
    piece = (PARTS, fine, rows)
    out_shape = (
        shape((rows, chans), BF16),
        shape((rows, chans), BF16),
        shape((rows, chans), BF16),
        shape((rows, chans), F32),
        shape(out_weight.shape, F32),
    )
    anywhere = pl.BlockSpec(memory_space=pl.ANY)
    results = pl.pallas_call(
        whole,
        out_shape=out_shape,
        in_specs=[anywhere] * 12,
        out_specs=(anywhere,) * 5,
        scratch_shapes=[
            block,
            block,
            block,
            pltpu.VMEM((rows, chans), F32),
            pltpu.VMEM((1, chans), F32),
            *(pltpu.VMEM(t.shape, t.dtype) for t in tables),
            *(pltpu.VMEM(o.shape, o.dtype) for o in out_shape),
            *(pltpu.VMEM((2, *t.shape), BF16) for t in tables[:4]),
            pltpu.VMEM((PARTS, chans, columns), BF16),
            pltpu.VMEM((WIDE, rows, chans), BF16),
            pltpu.VMEM((WIDE, 4, rows, columns), BF16),
            pltpu.VMEM((16, chans, rows), BF16),
            pltpu.VMEM((chans, rows), F32),
            pltpu.VMEM((PARTS, 2 * fine, rows), BF16),
            pltpu.VMEM((PARTS, 2 * fine, rows), BF16),
            pltpu.VMEM(piece, BF16),
            pltpu.VMEM(piece, BF16),
            pltpu.VMEM(piece, BF16),
            pltpu.VMEM(piece, BF16),
            pltpu.VMEM((PARTS, 2 * fine, rows), BF16),
            pltpu.VMEM((PARTS, 2 * fine, rows), BF16),
            pltpu.VMEM((chans, rows), F32),
            pltpu.VMEM((chans, columns), BF16),
            pltpu.VMEM((chans, columns), BF16),
            pltpu.SemaphoreType.DMA((12,)),
            pltpu.SemaphoreType.DMA((5,)),
            pltpu.SemaphoreType.DMA((6,)),
            pltpu.SemaphoreType.DMA((71,)),
            pltpu.SemaphoreType.DMA((4,)),
            pltpu.SemaphoreType.DMA((4,)),
        ],
        compiler_params=pltpu.CompilerParams(
            collective_id=0, has_side_effects=True, vmem_limit_bytes=63 * 2**20
        ),
        name="whole",
    )(
        query, key, value, filter_raw, rates.reshape(1, chans), out_weight, cotangent,
        *(jnp.asarray(t) for t in tables),
    )
    return pl.pallas_call(
        hand_over,
        out_shape=out_shape,
        in_specs=[anywhere] * 5,
        out_specs=(anywhere,) * 5,
        scratch_shapes=[pltpu.VMEM(o.shape, o.dtype) for o in out_shape]
        + [pltpu.SemaphoreType.DMA((5,)), pltpu.SemaphoreType.DMA((5,))],
        compiler_params=pltpu.CompilerParams(vmem_limit_bytes=63 * 2**20),
        name="hand_over",
    )(*results)


def solution(mesh):
    return jax.shard_map(
        on_device,
        mesh=mesh,
        in_specs=(
            P("seq", "ch"),
            P("seq", "ch"),
            P("seq", "ch"),
            P("seq", "ch"),
            P("ch"),
            P("ch", "seq"),
            P("seq", "ch"),
        ),
        out_specs=(P("seq", "ch"), P("seq", "ch"), P("seq", "ch"), P("seq", "ch"), P("ch", "seq")),
        check_vma=False,
    )
```
